32 devices in a mesh: pano: 2 (over y), seq: 4 (over z), win: 4 (over x, core).
Axes of the slice: x: 2, y: 2, z: 4, core: 2. Of those that a mesh axis runs over, the one named last changes fastest.
Arguments:
- query: bfloat16 [8, 768, 1536], P(('pano', 'win'), 'seq'), parts along dimension 0, may hold values from -8 to 8
- key_image: bfloat16 [8, 768, 1536], P(('pano', 'win'), 'seq'), parts along dimension 0, may hold values from -8 to 8
- value_image: bfloat16 [8, 768, 1536], P(('pano', 'win'), 'seq'), parts along dimension 0, may hold values from -6 to 6
- key_text: bfloat16 [8, 64, 1536], P(('pano', 'win'), 'seq'), parts along dimension 0, may hold values from -6 to 6
- value_text: bfloat16 [8, 64, 1536], P(('pano', 'win'), 'seq'), parts along dimension 0, may hold values from -6 to 6
- prompt_ids: int32 [8, 64], P(('pano', 'win')), parts along dimension 0, may hold values from 0 to 32127, as said below
- blend: int32 [8, 768], P(('pano', 'win'), 'seq'), parts along dimension 0, may hold values from 1 to 15, as said below
- w_out: bfloat16 [1536, 3072], replicated, may hold values from -0.15625 to 0.15625
Outputs:
- joined: bfloat16 [8, 768, 3072], P(('pano', 'win'), 'seq'), parts along dimension 0
The draws below stay inside these ranges and needn't reach their ends.
There are 2 independent parts, one for each index of `pano`. The reference program is written for one: setup_inputs(seed, part) draws one part's arguments, and reference() takes and returns one part's arrays. A program takes and returns all parts, laid end to end along the dimension named above; an argument that names none is the same for every part. Nothing has to cross between parts.
Inputs may be any that keep to these rules, and one draw needn't show every extreme that they name: `prompt_ids`: in each window the nonzero ids form a leading run of 16 or more positions and the rest are 0. At row r and column c < 32, blend[w] plus blend[w - 1] at row r, column c + 32 equals 16, window numbers taken modulo 4.
All inputs are finite; a program needn't handle non-finite values.
Results may differ from the reference program's by a relative error of at most 0.0085.
Values may be sent and summed in bfloat16 or wider, within the bound.
No kernel may reach another device: no remote copies, remote signals or barrier semaphores. Data moves between devices by JAX's collectives and lax.ppermute only.
A program may use at most 64 MiB of HBM per device.

```python
import jax
import jax.numpy as jnp
from jax import lax

D = 3072
HEADS = 12
HEAD_DIM = 128
VOCAB = 32128
WCOLS = 64
STRIDE = 32
WROWS = 12
IMG = 768
TXT = 64
HD = 1536
WINDOWS = 4


def draw_query(key, part):
    shape_full = (WINDOWS, IMG, HEADS * HEAD_DIM)
    values = jnp.clip(2.5 * jax.random.normal(jax.random.fold_in(key, 23), shape_full, jnp.float32), -8.0, 8.0)
    return values.astype(jnp.bfloat16)


def draw_key_image(key, part):
    shape_full = (WINDOWS, IMG, HEADS * HEAD_DIM)
    values = jnp.clip(jax.random.normal(jax.random.fold_in(key, 33), shape_full, jnp.float32), -6.0, 6.0)
    return values.astype(jnp.bfloat16)


def draw_prompt_ids(key, part):
    lengths = jax.random.randint(jax.random.fold_in(key, 41), (WINDOWS, 1), TXT // 4, TXT + 1)
    tokens = jax.random.randint(jax.random.fold_in(key, 42), (WINDOWS, TXT), 1, VOCAB)
    position = jnp.arange(TXT)[None, :]
    return jnp.where(position < lengths, tokens, 0).astype(jnp.int32)


def draw_blend(key, part):
    ramps = jax.random.randint(jax.random.fold_in(key, 51), (WINDOWS, WROWS, STRIDE), 1, 16)
    left_part = jnp.roll(ramps, 1, axis=0)
    right_part = 16 - ramps
    return jnp.concatenate([left_part, right_part], axis=2).reshape(WINDOWS, IMG).astype(jnp.int32)


def level_of(rng, dims, pieces, low, high):
    def one(axis_at, blocks):
        heights = jax.random.uniform(jax.random.fold_in(jax.random.fold_in(rng, 6), axis_at), (blocks,), jnp.float32, low / len(pieces), high / len(pieces))
        return jnp.repeat(jnp.exp(heights), dims[axis_at] // blocks).reshape((-1,) + (1,) * (len(dims) - axis_at - 1))

    loudness = one(*pieces[0])
    for cut in pieces[1:]:
        loudness = loudness * one(*cut)
    return loudness


def gaussian(rng, extent, spread, limit, shards=(), kind=jnp.bfloat16):
    array = jax.random.normal(rng, extent, jnp.float32) * spread
    if len(shards) > 0:
        array = level_of(rng, extent, shards, -0.22, 0.18) * array
    return jnp.clip(array, min=-limit, max=limit).astype(kind)


def setup_inputs(seed: int = 0, part: int = 0) -> dict:
    streams_of = jax.random.split(jax.random.key(seed), 9)
    own_keys = jax.random.split(jax.random.fold_in(streams_of[8], part), 9)
    query = draw_query(jax.random.fold_in(jax.random.fold_in(streams_of[8], part), 71), part)
    key_image = draw_key_image(jax.random.fold_in(jax.random.fold_in(streams_of[8], part), 71), part)
    value_image = gaussian(own_keys[2], (WINDOWS, IMG, HD), 1.0, 6.0, ((0, 4), (1, 4)))
    key_text = gaussian(own_keys[3], (WINDOWS, TXT, HD), 1.0, 6.0, ((0, 4), (1, 4)))
    value_text = gaussian(own_keys[4], (WINDOWS, TXT, HD), 1.0, 6.0, ((0, 4), (1, 4)))
    prompt_ids = draw_prompt_ids(jax.random.fold_in(jax.random.fold_in(streams_of[8], part), 71), part)
    blend = draw_blend(jax.random.fold_in(jax.random.fold_in(streams_of[8], part), 71), part)
    w_out = gaussian(streams_of[7], (HD, D), HD ** -0.5, 0.15625)
    return dict(query=query, key_image=key_image, value_image=value_image, key_text=key_text, value_text=value_text, prompt_ids=prompt_ids, blend=blend, w_out=w_out)


blend_total = 16.0


def attend_window(operands):
    query, key_image, value_image, key_text, value_text, prompt_ids = operands
    keys_all = jnp.concatenate([key_image, key_text], axis=0)
    values_all = jnp.concatenate([value_image, value_text], axis=0)
    valid_keys = jnp.concatenate([jnp.ones((IMG,), jnp.bool_), prompt_ids != 0])

    def one_head(head_index):
        offset = (head_index * HEAD_DIM).astype(jnp.int32)
        query_head = lax.dynamic_slice_in_dim(query, offset, HEAD_DIM, 1)
        key_head = lax.dynamic_slice_in_dim(keys_all, offset, HEAD_DIM, 1)
        value_head = lax.dynamic_slice_in_dim(values_all, offset, HEAD_DIM, 1)
        scores = jnp.dot(query_head, key_head.T, preferred_element_type=jnp.float32) * (HEAD_DIM ** -0.5)
        scores = jnp.where(valid_keys[None, :], scores, -jnp.inf)
        peak = jnp.max(scores, axis=1, keepdims=True)
        weights = jnp.exp(scores - peak)
        total = jnp.sum(weights, axis=1, keepdims=True)
        return jnp.dot(weights.astype(jnp.bfloat16), value_head, preferred_element_type=jnp.float32) / total

    heads_out = lax.map(one_head, jnp.arange(HEADS, dtype=jnp.int32))
    return jnp.transpose(heads_out, (1, 0, 2)).reshape(IMG, HD).astype(jnp.bfloat16)


def reference(query, key_image, value_image, key_text, value_text, prompt_ids, blend, w_out):
    attended = lax.map(attend_window, (query, key_image, value_image, key_text, value_text, prompt_ids))
    projected = jnp.dot(attended.reshape(WINDOWS * IMG, HD), w_out, preferred_element_type=jnp.float32)
    projected = projected.astype(jnp.bfloat16).reshape(WINDOWS, WROWS, WCOLS, D)
    prev_right = jnp.roll(projected[:, :, STRIDE:], 1, axis=0)
    next_left = jnp.roll(projected[:, :, :STRIDE], -1, axis=0)
    partner = jnp.concatenate([prev_right, next_left], axis=2).astype(jnp.float32)
    weight_own = blend.reshape(WINDOWS, WROWS, WCOLS, 1).astype(jnp.float32)
    joined = (weight_own * projected.astype(jnp.float32) + (blend_total - weight_own) * partner) / blend_total
    return joined.astype(jnp.bfloat16).reshape(WINDOWS, IMG, D)
```

```python
import functools
import math

import jax
import jax.numpy as jnp
from jax import lax
from jax.experimental import pallas as pl
from jax.experimental.pallas import tpu as pltpu
from jax.sharding import PartitionSpec as P

HEADS = 12
HEAD_DIM = 128
WCOLS = 64
STRIDE = 32
BLEND_TOTAL = 16.0
SCALE = HEAD_DIM ** (-0.5)
EXP2_SCALE = SCALE * math.log2(math.e)
VMEM_LIMIT = 24 * 1024 * 1024

ANY = pl.BlockSpec(memory_space=pl.ANY)
VMEM = pl.BlockSpec(memory_space=pltpu.VMEM)


def shifted(block, axis, distance, group):
    count = lax.axis_size(axis)
    route = []
    for i in range(count):
        base = i // group * group
        route.append((i, base + (i % group + distance) % group))
    return lax.ppermute(block, axis, route)


def pack_kernel(chunk, group, head_count, *refs):
    sources, packed, sems = refs[:5], refs[5 : 5 + group], refs[5 + group]
    position = lax.rem(lax.axis_index("seq"), group)
    copies = []
    for distance in range(group):
        head = lax.rem(position + distance, group) * head_count + chunk
        columns = pl.ds(pl.multiple_of(head * HEAD_DIM, HEAD_DIM), HEAD_DIM)
        row = 0
        for source in sources:
            rows = source.shape[0]
            copy = pltpu.make_async_copy(
                source.at[:, columns], packed[distance].at[pl.ds(row, rows)], sems.at[len(copies)]
            )
            copy.start()
            copies.append(copy)
            row += rows
    for copy in copies:
        copy.wait()


def pack(sources, chunk, group, head_count):
    rows = sum(source.shape[0] for source in sources)
    return pl.pallas_call(
        functools.partial(pack_kernel, chunk, group, head_count),
        out_shape=[jax.ShapeDtypeStruct((rows, HEAD_DIM), sources[0].dtype)] * group,
        in_specs=[ANY] * len(sources),
        out_specs=[ANY] * group,
        scratch_shapes=[pltpu.SemaphoreType.DMA((group * len(sources),))],
        name="pack",
    )(*sources)


def attend_kernel(group, image_rows, text_rows, ids, *refs):
    blocks, (left, right, keys, values) = refs[:group], refs[group:]
    position = lax.rem(lax.axis_index("seq"), group)
    key_rows = image_rows + text_rows
    for distance in range(group):
        block = blocks[distance]
        source = lax.rem(position - distance + group, group)
        image = pl.ds(distance * image_rows, image_rows)
        text = pl.ds(pl.multiple_of(group * image_rows + source * text_rows, text_rows), text_rows)
        key_at, value_at = image_rows, image_rows + key_rows
        keys[image] = block[key_at : key_at + image_rows]
        keys[text] = block[key_at + image_rows : key_at + key_rows]
        values[image] = block[value_at : value_at + image_rows]
        values[text] = block[value_at + image_rows : value_at + key_rows]
    image_keys = group * image_rows
    valid = ids[...] != 0
    half = left.shape[0] // group
    for distance in range(group):
        scores = lax.dot_general(
            blocks[distance][:image_rows],
            keys[...],
            (((1,), (1,)), ((), ())),
            preferred_element_type=jnp.float32,
        )
        scores = jnp.concatenate(
            [scores[:, :image_keys], jnp.where(valid, scores[:, image_keys:], -jnp.inf)], axis=1
        )
        peak = jnp.max(scores, axis=1, keepdims=True)
        weights = jnp.exp2((scores - peak) * EXP2_SCALE)
        total = jnp.sum(weights, axis=1, keepdims=True)
        result = jnp.dot(
            weights.astype(jnp.bfloat16), values[...], preferred_element_type=jnp.float32
        )
        result = (result / total).astype(jnp.bfloat16)
        for row in range(image_rows // WCOLS):
            at = distance * half + row * STRIDE
            left[at : at + STRIDE] = result[row * WCOLS : row * WCOLS + STRIDE]
            right[at : at + STRIDE] = result[row * WCOLS + STRIDE : (row + 1) * WCOLS]


def attend(blocks, ids, image_rows, text_rows):
    group = len(blocks)
    strip = jax.ShapeDtypeStruct((group * image_rows // 2, HEAD_DIM), jnp.bfloat16)
    keys = pltpu.VMEM((group * (image_rows + text_rows), HEAD_DIM), jnp.bfloat16)
    key_count, query_count = group * (image_rows + text_rows), group * image_rows
    return pl.pallas_call(
        functools.partial(attend_kernel, group, image_rows, text_rows),
        out_shape=[strip, strip],
        in_specs=[VMEM] * (1 + group),
        out_specs=[VMEM, VMEM],
        scratch_shapes=[keys, keys],
        compiler_params=pltpu.CompilerParams(vmem_limit_bytes=VMEM_LIMIT),
        cost_estimate=pl.CostEstimate(
            flops=4 * query_count * key_count * HEAD_DIM,
            bytes_accessed=4 * key_count * HEAD_DIM * 2,
            transcendentals=query_count * key_count,
        ),
        name="attend",
    )(ids, *blocks)


def blend_kernel(group, left, right, from_prev, from_next, weight_left, weight_right, *outs):
    half = left.shape[0] // group
    for own, partner, weight_ref, at in (
        (left, from_prev, weight_left, 0),
        (right, from_next, weight_right, half),
    ):
        for distance in range(group):
            rows = pl.ds(distance * half, half)
            weight = weight_ref[rows]
            mixed = weight * own[rows].astype(jnp.float32) + (BLEND_TOTAL - weight) * partner[
                rows
            ].astype(jnp.float32)
            outs[distance][pl.ds(at, half)] = (mixed * (1.0 / BLEND_TOTAL)).astype(jnp.bfloat16)


def blend_strips(left, right, from_prev, from_next, weight_left, weight_right, group):
    out = jax.ShapeDtypeStruct((2 * left.shape[0] // group, HEAD_DIM), jnp.bfloat16)
    return pl.pallas_call(
        functools.partial(blend_kernel, group),
        out_shape=[out] * group,
        in_specs=[VMEM] * 6,
        out_specs=[VMEM] * group,
        name="blend",
    )(left, right, from_prev, from_next, weight_left, weight_right)


def project_kernel(group, head_count, *refs):
    blocks, (w_out, out, features) = refs[: group * head_count], refs[group * head_count :]
    image_rows = out.shape[0]

    @pl.when(pl.program_id(0) == 0)
    def _():
        position = lax.rem(lax.axis_index("seq"), group)
        for chunk in range(head_count):
            for distance in range(group):
                head = lax.rem(position + distance, group) * head_count + chunk
                columns = pl.ds(pl.multiple_of(head * HEAD_DIM, HEAD_DIM), HEAD_DIM)
                block = blocks[chunk * group + distance]
                for row in range(image_rows // WCOLS):
                    for side in range(2):
                        start = side * image_rows // 2 + row * STRIDE
                        features[pl.ds(row * WCOLS + side * STRIDE, STRIDE), columns] = block[
                            start : start + STRIDE
                        ]

    out[...] = jnp.dot(features[...], w_out[...], preferred_element_type=jnp.float32).astype(
        jnp.bfloat16
    )


def project(blocks, w_out, group, head_count):
    image_rows = blocks[0].shape[0]
    depth, width = w_out.shape
    tile = width // 6
    return pl.pallas_call(
        functools.partial(project_kernel, group, head_count),
        grid=(width // tile,),
        out_shape=jax.ShapeDtypeStruct((image_rows, width), jnp.bfloat16),
        in_specs=[pl.BlockSpec((image_rows, HEAD_DIM), lambda n: (0, 0))] * len(blocks)
        + [pl.BlockSpec((depth, tile), lambda n: (0, n))],
        out_specs=pl.BlockSpec((image_rows, tile), lambda n: (0, n)),
        scratch_shapes=[pltpu.VMEM((image_rows, depth), jnp.bfloat16)],
        compiler_params=pltpu.CompilerParams(vmem_limit_bytes=VMEM_LIMIT),
        cost_estimate=pl.CostEstimate(
            flops=2 * image_rows * depth * width,
            bytes_accessed=2 * (depth * width + image_rows * (depth + width)),
            transcendentals=0,
        ),
        name="project",
    )(*blocks, w_out)


def absorb(carried, keys, values, valid_keys, queries):
    running, denominator, numerator = carried
    scores = jnp.einsum("qhd,khd->qhk", queries, keys, preferred_element_type=jnp.float32) * SCALE
    scores = jnp.where(valid_keys[None, None, :], scores, -jnp.inf)
    updated = jnp.maximum(running, jnp.max(scores, axis=2))
    rescale = jnp.exp(running - updated)
    weights = jnp.exp(scores - updated[:, :, None])
    denominator = denominator * rescale + jnp.sum(weights, axis=2)
    product = jnp.einsum(
        "qhk,khd->qhd", weights.astype(jnp.bfloat16), values, preferred_element_type=jnp.float32
    )
    numerator = numerator * rescale[:, :, None] + product
    return (updated, denominator, numerator)


def attend_ring(blocks, prompt_ids, image_rows, text_rows):
    head_count, group = len(blocks), len(blocks[0])
    key_rows = image_rows + text_rows
    stacked = jnp.stack([jnp.stack(chunk) for chunk in blocks], axis=2)
    queries = stacked[:, :image_rows].reshape(group * image_rows, head_count, HEAD_DIM)
    keys = stacked[:, image_rows : image_rows + key_rows].reshape(-1, head_count, HEAD_DIM)
    values = stacked[:, image_rows + key_rows :].reshape(-1, head_count, HEAD_DIM)
    seq_count = lax.axis_size("seq")
    group_count = seq_count // group
    own_group = lax.axis_index("seq") // group
    order = (lax.axis_index("seq") % group - jnp.arange(group)) % group
    text_valid = prompt_ids.reshape(seq_count, text_rows) != 0

    def valid_for(source):
        text = lax.dynamic_slice_in_dim(text_valid, source * group, group, 0)[order]
        return jnp.concatenate([jnp.ones((group, image_rows), jnp.bool_), text], axis=1).reshape(-1)

    def next_group(block):
        route = [(i, (i + group) % seq_count) for i in range(seq_count)]
        return lax.ppermute(block, "seq", route)

    query_count = group * image_rows
    initial = (
        jnp.full((query_count, head_count), -jnp.inf, jnp.float32),
        jnp.zeros((query_count, head_count), jnp.float32),
        jnp.zeros((query_count, head_count, HEAD_DIM), jnp.float32),
    )
    carried = absorb(initial, keys, values, valid_for(own_group), queries)

    def one_turn(turn, state):
        current, keys, values = state
        keys, values = next_group(keys), next_group(values)
        source = (own_group - turn) % group_count
        return (absorb(current, keys, values, valid_for(source), queries), keys, values)

    carried, _, _ = lax.fori_loop(1, group_count, one_turn, (carried, keys, values))
    _, denominator, numerator = carried
    attended = (numerator / denominator[:, :, None]).astype(jnp.bfloat16)
    sides = attended.reshape(-1, 2, STRIDE, head_count, HEAD_DIM)
    return [
        (sides[:, 0, :, c].reshape(-1, HEAD_DIM), sides[:, 1, :, c].reshape(-1, HEAD_DIM))
        for c in range(head_count)
    ]


def on_device(query, key_image, value_image, key_text, value_text, prompt_ids, blend, w_out):
    seq_count = lax.axis_size("seq")
    win_count = lax.axis_size("win")
    group = math.gcd(HEADS, seq_count)
    head_count = HEADS // group
    image_rows, text_rows = query.shape[1], key_text.shape[1]
    sources = [query[0], key_image[0], key_text[0], value_image[0], value_text[0]]

    blocks = []
    for chunk in range(head_count):
        packed = pack(sources, chunk, group, head_count)
        blocks.append(
            [packed[0]] + [shifted(packed[d], "seq", d, group) for d in range(1, group)]
        )

    weights = jnp.concatenate(
        [blend] + [shifted(blend, "seq", d, group) for d in range(1, group)], axis=0
    )
    weights = weights.astype(jnp.float32).reshape(-1, 2, STRIDE)
    weight_left, weight_right = (weights[:, side].reshape(-1, 1) for side in range(2))

    if seq_count == group:
        strips = [attend(chunk, prompt_ids, image_rows, text_rows) for chunk in blocks]
    else:
        strips = attend_ring(blocks, prompt_ids[0], image_rows, text_rows)

    features = []
    for left, right in strips:
        from_prev = shifted(right, "win", 1, win_count)
        from_next = shifted(left, "win", -1, win_count)
        mixed = blend_strips(left, right, from_prev, from_next, weight_left, weight_right, group)
        features.append(mixed[0])
        features += [shifted(mixed[d], "seq", -d, group) for d in range(1, group)]
    return project(features, w_out, group, head_count)[None]


def solution(mesh):
    tokens = P(("pano", "win"), "seq", None)
    return jax.shard_map(
        on_device,
        mesh=mesh,
        in_specs=(tokens,) * 5 + (P(("pano", "win"), None), P(("pano", "win"), "seq"), P()),
        out_specs=tokens,
        check_vma=False,
    )
```

```python
import functools
import math

import jax
import jax.numpy as jnp
from jax import lax
from jax.experimental import pallas as pl
from jax.experimental.pallas import tpu as pltpu
from jax.sharding import PartitionSpec as P

HEADS = 12
HEAD_DIM = 128
WCOLS = 64
STRIDE = 32
BLEND_TOTAL = 16.0
SCALE = HEAD_DIM ** (-0.5)
EXP2_SCALE = SCALE * math.log2(math.e)
SMALL = pltpu.CompilerParams(vmem_limit_bytes=16 * 1024 * 1024)

ANY = pl.BlockSpec(memory_space=pl.ANY)
HBM = pl.BlockSpec(memory_space=pltpu.HBM)
VMEM = pl.BlockSpec(memory_space=pltpu.VMEM)


def shifted(block, axis, distance, group):
    count = lax.axis_size(axis)
    route = []
    for i in range(count):
        base = i // group * group
        route.append((i, base + (i % group + distance) % group))
    return lax.ppermute(block, axis, route)


def pack_kernel(chunk, group, head_count, count, *refs):
    sources, packed, sems = refs[:count], refs[count : count + group], refs[count + group]
    position = lax.rem(lax.axis_index("seq"), group)
    copies = []
    for distance in range(group):
        head = lax.rem(position + distance, group) * head_count + chunk
        columns = pl.ds(pl.multiple_of(head * HEAD_DIM, HEAD_DIM), HEAD_DIM)
        row = 0
        for source in sources:
            rows = source.shape[0]
            narrow = source.shape[1] == HEAD_DIM
            copy = pltpu.make_async_copy(
                source if narrow else source.at[:, columns],
                packed[distance].at[pl.ds(row, rows)],
                sems.at[len(copies)],
            )
            copy.start()
            copies.append(copy)
            row += rows
    for copy in copies:
        copy.wait()


def pack(sources, chunk, group, head_count):
    rows = sum(source.shape[0] for source in sources)
    return pl.pallas_call(
        functools.partial(pack_kernel, chunk, group, head_count, len(sources)),
        out_shape=[jax.ShapeDtypeStruct((rows, HEAD_DIM), sources[0].dtype)] * group,
        in_specs=[HBM] * len(sources),
        out_specs=[VMEM] * group,
        scratch_shapes=[pltpu.SemaphoreType.DMA((group * len(sources),))],
        compiler_params=SMALL,
        name="pack",
    )(*sources)


def attend_kernel(group, image_rows, text_rows, ids, *refs):
    blocks, (left, right, keys, values) = refs[:group], refs[group:]
    position = lax.rem(lax.axis_index("seq"), group)
    key_rows = image_rows + text_rows
    for distance in range(group):
        block = blocks[distance]
        source = lax.rem(position - distance + group, group)
        image = pl.ds(distance * image_rows, image_rows)
        text = pl.ds(pl.multiple_of(group * image_rows + source * text_rows, text_rows), text_rows)
        key_at, value_at = image_rows, image_rows + key_rows
        keys[image] = block[key_at : key_at + image_rows]
        keys[text] = block[key_at + image_rows : key_at + key_rows]
        values[image] = block[value_at : value_at + image_rows]
        values[text] = block[value_at + image_rows : value_at + key_rows]
    image_keys = group * image_rows
    valid = ids[...] != 0
    half = left.shape[0] // group
    for distance in range(group):
        scores = lax.dot_general(
            blocks[distance][:image_rows],
            keys[...],
            (((1,), (1,)), ((), ())),
            preferred_element_type=jnp.float32,
        )
        scores = jnp.concatenate(
            [scores[:, :image_keys], jnp.where(valid, scores[:, image_keys:], -jnp.inf)], axis=1
        )
        peak = jnp.max(scores, axis=1, keepdims=True)
        weights = jnp.exp2((scores - peak) * EXP2_SCALE)
        total = jnp.sum(weights, axis=1, keepdims=True)
        result = jnp.dot(
            weights.astype(jnp.bfloat16), values[...], preferred_element_type=jnp.float32
        )
        result = (result / total).astype(jnp.bfloat16)
        for row in range(image_rows // WCOLS):
            at = distance * half + row * STRIDE
            left[at : at + STRIDE] = result[row * WCOLS : row * WCOLS + STRIDE]
            right[at : at + STRIDE] = result[row * WCOLS + STRIDE : (row + 1) * WCOLS]


def attend(blocks, ids, image_rows, text_rows):
    group = len(blocks)
    strip = jax.ShapeDtypeStruct((group * image_rows // 2, HEAD_DIM), jnp.bfloat16)
    keys = pltpu.VMEM((group * (image_rows + text_rows), HEAD_DIM), jnp.bfloat16)
    key_count, query_count = group * (image_rows + text_rows), group * image_rows
    return pl.pallas_call(
        functools.partial(attend_kernel, group, image_rows, text_rows),
        out_shape=[strip, strip],
        in_specs=[VMEM] * (1 + group),
        out_specs=[VMEM, VMEM],
        scratch_shapes=[keys, keys],
        compiler_params=SMALL,
        cost_estimate=pl.CostEstimate(
            flops=4 * query_count * key_count * HEAD_DIM,
            bytes_accessed=4 * key_count * HEAD_DIM * 2,
            transcendentals=query_count * key_count,
        ),
        name="attend",
    )(ids, *blocks)


def weigh_kernel(group, weight_row, image_rows, *refs):
    blocks, (weight_left, weight_right) = refs[:group], refs[group:]
    half = image_rows // 2
    for distance in range(group):
        columns = blocks[distance][weight_row : weight_row + 16].astype(jnp.float32).T
        for row in range(image_rows // WCOLS):
            column, start = row * WCOLS // 128, row * WCOLS % 128
            at = distance * half + row * STRIDE
            for side, out in ((0, weight_left), (1, weight_right)):
                first = start + side * STRIDE
                out[at : at + STRIDE] = jnp.broadcast_to(
                    columns[first : first + STRIDE, column : column + 1], (STRIDE, HEAD_DIM)
                )


def weigh(blocks, weight_row, image_rows):
    group = len(blocks)
    out = jax.ShapeDtypeStruct((group * image_rows // 2, HEAD_DIM), jnp.float32)
    return pl.pallas_call(
        functools.partial(weigh_kernel, group, weight_row, image_rows),
        out_shape=[out, out],
        in_specs=[VMEM] * group,
        out_specs=[VMEM, VMEM],
        compiler_params=SMALL,
        name="weigh",
    )(*blocks)


def blend_kernel(group, left, right, from_prev, from_next, weight_left, weight_right, *outs):
    half = left.shape[0] // group
    for own, partner, weight_ref, at in (
        (left, from_prev, weight_left, 0),
        (right, from_next, weight_right, half),
    ):
        for distance in range(group):
            rows = pl.ds(distance * half, half)
            weight = weight_ref[rows]
            mixed = weight * own[rows].astype(jnp.float32) + (BLEND_TOTAL - weight) * partner[
                rows
            ].astype(jnp.float32)
            outs[distance][pl.ds(at, half)] = (mixed * (1.0 / BLEND_TOTAL)).astype(jnp.bfloat16)


def blend_strips(left, right, from_prev, from_next, weight_left, weight_right, group):
    out = jax.ShapeDtypeStruct((2 * left.shape[0] // group, HEAD_DIM), jnp.bfloat16)
    return pl.pallas_call(
        functools.partial(blend_kernel, group),
        out_shape=[out] * group,
        in_specs=[VMEM] * 6,
        out_specs=[VMEM] * group,
        compiler_params=SMALL,
        name="blend",
    )(left, right, from_prev, from_next, weight_left, weight_right)


def load_kernel(group, head_count, w_out, *refs):
    outs, sems = refs[:head_count], refs[head_count]
    copies = []
    for chunk in range(head_count):
        for source in range(group):
            head = source * head_count + chunk
            copy = pltpu.make_async_copy(
                w_out.at[pl.ds(head * HEAD_DIM, HEAD_DIM)],
                outs[chunk].at[pl.ds(source * HEAD_DIM, HEAD_DIM)],
                sems.at[len(copies)],
            )
            copy.start()
            copies.append(copy)
    for copy in copies:
        copy.wait()


def load_weights(w_out, group, head_count):
    out = jax.ShapeDtypeStruct((group * HEAD_DIM, w_out.shape[1]), w_out.dtype)
    return pl.pallas_call(
        functools.partial(load_kernel, group, head_count),
        out_shape=[out] * head_count,
        in_specs=[ANY],
        out_specs=[VMEM] * head_count,
        scratch_shapes=[pltpu.SemaphoreType.DMA((group * head_count,))],
        compiler_params=SMALL,
        name="load_weights",
    )(w_out)


def gather_features(blocks, features):
    group, image_rows = len(blocks), features.shape[0]
    position = lax.rem(lax.axis_index("seq"), group)
    for distance, block in enumerate(blocks):
        source = lax.rem(position + distance, group)
        columns = pl.ds(pl.multiple_of(source * HEAD_DIM, HEAD_DIM), HEAD_DIM)
        for row in range(image_rows // WCOLS):
            for side in range(2):
                start = side * image_rows // 2 + row * STRIDE
                at = row * WCOLS + side * STRIDE
                features[pl.ds(at, STRIDE), columns] = block[start : start + STRIDE]


def begin_kernel(group, count, *refs):
    blocks, weights = refs[: group * count], refs[group * count : (group + 1) * count]
    total = refs[(group + 1) * count]
    features = refs[(group + 1) * count + 1 :]
    for chunk in range(count):
        gather_features(blocks[chunk * group : (chunk + 1) * group], features[chunk])
    tile = total.shape[1] // 6
    for at in range(0, total.shape[1], tile):
        total[:, at : at + tile] = sum(
            jnp.dot(
                features[chunk][...],
                weights[chunk][:, at : at + tile],
                preferred_element_type=jnp.float32,
            )
            for chunk in range(count)
        )


def project_begin(blocks, weights, group):
    image_rows, width = blocks[0].shape[0], weights[0].shape[1]
    count = len(weights)
    return pl.pallas_call(
        functools.partial(begin_kernel, group, count),
        out_shape=jax.ShapeDtypeStruct((image_rows, width), jnp.float32),
        in_specs=[VMEM] * (len(blocks) + count),
        out_specs=VMEM,
        scratch_shapes=[pltpu.VMEM((image_rows, group * HEAD_DIM), jnp.bfloat16)] * count,
        compiler_params=SMALL,
        name="project_begin",
    )(*blocks, *weights)


def end_kernel(group, *refs):
    blocks, (weights, total, out, features, result, sems) = refs[:group], refs[group:]
    gather_features(blocks, features)
    tile = result.shape[1] // 6
    copies = []
    for at in range(0, result.shape[1], tile):
        columns = pl.ds(at, tile)
        product = jnp.dot(
            features[...], weights[:, columns], preferred_element_type=jnp.float32
        )
        result[:, columns] = (total[:, columns] + product).astype(jnp.bfloat16)
        copy = pltpu.make_async_copy(
            result.at[:, columns], out.at[:, columns], sems.at[len(copies)]
        )
        copy.start()
        copies.append(copy)
    for copy in copies:
        copy.wait()


def project_end(blocks, weights, total, group):
    image_rows, width = total.shape
    return pl.pallas_call(
        functools.partial(end_kernel, group),
        out_shape=jax.ShapeDtypeStruct((image_rows, width), jnp.bfloat16),
        in_specs=[VMEM] * (len(blocks) + 2),
        out_specs=ANY,
        scratch_shapes=[
            pltpu.VMEM((image_rows, group * HEAD_DIM), jnp.bfloat16),
            pltpu.VMEM((image_rows, width), jnp.bfloat16),
            pltpu.SemaphoreType.DMA((6,)),
        ],
        compiler_params=SMALL,
        name="project_end",
    )(*blocks, weights, total)


def absorb(carried, keys, values, valid_keys, queries):
    running, denominator, numerator = carried
    scores = jnp.einsum("qhd,khd->qhk", queries, keys, preferred_element_type=jnp.float32) * SCALE
    scores = jnp.where(valid_keys[None, None, :], scores, -jnp.inf)
    updated = jnp.maximum(running, jnp.max(scores, axis=2))
    rescale = jnp.exp(running - updated)
    weights = jnp.exp(scores - updated[:, :, None])
    denominator = denominator * rescale + jnp.sum(weights, axis=2)
    product = jnp.einsum(
        "qhk,khd->qhd", weights.astype(jnp.bfloat16), values, preferred_element_type=jnp.float32
    )
    numerator = numerator * rescale[:, :, None] + product
    return (updated, denominator, numerator)


def attend_ring(blocks, prompt_ids, image_rows, text_rows):
    head_count, group = len(blocks), len(blocks[0])
    key_rows = image_rows + text_rows
    stacked = jnp.stack([jnp.stack(chunk) for chunk in blocks], axis=2)
    queries = stacked[:, :image_rows].reshape(group * image_rows, head_count, HEAD_DIM)
    keys = stacked[:, image_rows : image_rows + key_rows].reshape(-1, head_count, HEAD_DIM)
    values = stacked[:, image_rows + key_rows :].reshape(-1, head_count, HEAD_DIM)
    seq_count = lax.axis_size("seq")
    group_count = seq_count // group
    own_group = lax.axis_index("seq") // group
    order = (lax.axis_index("seq") % group - jnp.arange(group)) % group
    text_valid = prompt_ids.reshape(seq_count, text_rows) != 0

    def valid_for(source):
        text = lax.dynamic_slice_in_dim(text_valid, source * group, group, 0)[order]
        return jnp.concatenate([jnp.ones((group, image_rows), jnp.bool_), text], axis=1).reshape(-1)

    def next_group(block):
        route = [(i, (i + group) % seq_count) for i in range(seq_count)]
        return lax.ppermute(block, "seq", route)

    query_count = group * image_rows
    initial = (
        jnp.full((query_count, head_count), -jnp.inf, jnp.float32),
        jnp.zeros((query_count, head_count), jnp.float32),
        jnp.zeros((query_count, head_count, HEAD_DIM), jnp.float32),
    )
    carried = absorb(initial, keys, values, valid_for(own_group), queries)

    def one_turn(turn, state):
        current, keys, values = state
        keys, values = next_group(keys), next_group(values)
        source = (own_group - turn) % group_count
        return (absorb(current, keys, values, valid_for(source), queries), keys, values)

    carried, _, _ = lax.fori_loop(1, group_count, one_turn, (carried, keys, values))
    _, denominator, numerator = carried
    attended = (numerator / denominator[:, :, None]).astype(jnp.bfloat16)
    sides = attended.reshape(-1, 2, STRIDE, head_count, HEAD_DIM)
    return [
        (sides[:, 0, :, c].reshape(-1, HEAD_DIM), sides[:, 1, :, c].reshape(-1, HEAD_DIM))
        for c in range(head_count)
    ]


def on_device(query, key_image, value_image, key_text, value_text, prompt_ids, blend, w_out):
    seq_count = lax.axis_size("seq")
    win_count = lax.axis_size("win")
    group = math.gcd(HEADS, seq_count)
    head_count = HEADS // group
    image_rows, text_rows = query.shape[1], key_text.shape[1]
    sources = [query[0], key_image[0], key_text[0], value_image[0], value_text[0]]

    weight_rows = -(-image_rows // (16 * 128)) * 16
    weight_block = jnp.pad(
        blend[0].astype(jnp.bfloat16), (0, weight_rows * 128 - image_rows)
    ).reshape(weight_rows, 128)
    weight_chunk = min(1, head_count - 1)
    message_rows = 3 * image_rows + 2 * text_rows

    blocks = []
    for chunk in range(head_count):
        extra = [weight_block] if chunk == weight_chunk else []
        packed = pack(sources + extra, chunk, group, head_count)
        blocks.append(
            [packed[0]] + [shifted(packed[d], "seq", d, group) for d in range(1, group)]
        )
    w_chunks = load_weights(w_out, group, head_count)
    weight_left, weight_right = weigh(blocks[weight_chunk], message_rows, image_rows)

    if seq_count == group:
        strips = [attend(chunk, prompt_ids, image_rows, text_rows) for chunk in blocks]
    else:
        trimmed = [[block[:message_rows] for block in chunk] for chunk in blocks]
        strips = attend_ring(trimmed, prompt_ids[0], image_rows, text_rows)

    features = []
    for left, right in strips:
        from_prev = shifted(right, "win", 1, win_count)
        from_next = shifted(left, "win", -1, win_count)
        mixed = blend_strips(left, right, from_prev, from_next, weight_left, weight_right, group)
        features.append(
            [mixed[0]] + [shifted(mixed[d], "seq", -d, group) for d in range(1, group)]
        )
    total = project_begin(sum(features[:-1], []), w_chunks[:-1], group)
    return project_end(features[-1], w_chunks[-1], total, group)[None]


def solution(mesh):
    tokens = P(("pano", "win"), "seq", None)
    return jax.shard_map(
        on_device,
        mesh=mesh,
        in_specs=(tokens,) * 5 + (P(("pano", "win"), None), P(("pano", "win"), "seq"), P()),
        out_specs=tokens,
        check_vma=False,
    )
```

```python
import functools
import math

import jax
import jax.numpy as jnp
from jax import lax
from jax.experimental import pallas as pl
from jax.experimental.pallas import tpu as pltpu
from jax.sharding import PartitionSpec as P

HEADS = 12
HEAD_DIM = 128
WCOLS = 64
STRIDE = 32
BLEND_TOTAL = 16.0
SCALE = HEAD_DIM ** (-0.5)
EXP2_SCALE = SCALE * math.log2(math.e)
MIB = 1024 * 1024
SMALL = pltpu.CompilerParams(vmem_limit_bytes=16 * MIB)
NO_COST = pl.CostEstimate(flops=0, bytes_accessed=0, transcendentals=0)
LARGE = pltpu.CompilerParams(vmem_limit_bytes=60 * MIB)

ANY = pl.BlockSpec(memory_space=pl.ANY)
VMEM = pl.BlockSpec(memory_space=pltpu.VMEM)


def shifted(block, axis, distance):
    count = lax.axis_size(axis)
    return lax.ppermute(block, axis, [(i, (i + distance) % count) for i in range(count)])


def swapped(block, distance):
    return lax.ppermute(block, "seq", [(i, i ^ distance) for i in range(lax.axis_size("seq"))])


def crossed(block, step, distance):
    wins, seqs = lax.axis_size("win"), lax.axis_size("seq")
    route = [
        (s * wins + w, (s ^ distance) * wins + (w + step) % wins)
        for s in range(seqs)
        for w in range(wins)
    ]
    return lax.ppermute(block, ("seq", "win"), route)


def partner(distance, group):
    position = lax.rem(lax.axis_index("seq"), group)
    result, bit = 0, 1
    while bit < group:
        own = lax.rem(lax.div(position, bit), 2)
        result = result + (1 - own if distance & bit else own) * bit
        bit *= 2
    return result


def start_block(sources, packed, start, sems):
    columns = pl.ds(pl.multiple_of(start * HEAD_DIM, HEAD_DIM), packed.shape[1])
    copies, row = [], 0
    for source in sources:
        rows = source.shape[0]
        copy = pltpu.make_async_copy(
            source.at[:, columns], packed.at[pl.ds(row, rows)], sems.at[len(copies)]
        )
        copy.start()
        copies.append(copy)
        row += rows
    return copies


def store_weights(blend, wide, packed, row):
    wide[...] = jnp.zeros_like(wide)
    wide[:, : blend.shape[1]] = blend[...].astype(jnp.float32)
    rows, width = packed.shape[0] - row, packed.shape[1]
    index = lax.broadcasted_iota(jnp.int32, (rows, 128), 0)
    value = jnp.zeros((rows, 128), jnp.float32)
    for at in range(0, wide.shape[1], 128):
        value = jnp.where(index == at // 128, wide[:, at : at + 128], value)
    packed[row:, :128] = value.astype(packed.dtype)
    if width > 128:
        packed[row:, 128:] = jnp.zeros((rows, width - 128), packed.dtype)


def pack_kernel(heads, group, distances, count, *refs):
    sources, blend = refs[:count], refs[count]
    packed = refs[count + 1 : count + 1 + len(distances)]
    sems, blend_rows, wide = refs[count + 1 + len(distances) :]
    copies = []
    load = pltpu.make_async_copy(blend, blend_rows, sems.at[len(distances), 0])
    load.start()
    for index, distance in enumerate(distances):
        start = partner(distance, group) * heads
        copies += start_block(sources, packed[index], start, sems.at[index])
    load.wait()
    message_rows = sum(source.shape[0] for source in sources)
    for ref in packed:
        store_weights(blend_rows, wide, ref, message_rows)
    for copy in copies:
        copy.wait()


def weight_rows(blend):
    return -(-blend.shape[1] // (16 * 128)) * 16


def wide_shape(blend):
    return (1, -(-blend.shape[1] // 128) * 128)


def pack(sources, blend, heads, group, distances):
    rows = sum(source.shape[0] for source in sources) + weight_rows(blend)
    out = jax.ShapeDtypeStruct((rows, heads * HEAD_DIM), sources[0].dtype)
    return pl.pallas_call(
        functools.partial(pack_kernel, heads, group, distances, len(sources)),
        out_shape=[out] * len(distances),
        in_specs=[ANY] * (len(sources) + 1),
        out_specs=[VMEM] * len(distances),
        scratch_shapes=[
            pltpu.SemaphoreType.DMA((len(distances) + 1, len(sources))),
            pltpu.VMEM(blend.shape, blend.dtype),
            pltpu.VMEM(wide_shape(blend), jnp.float32),
        ],
        compiler_params=LARGE,
        cost_estimate=NO_COST,
        name="pack",
    )(*sources, blend)


def prepare_kernel(heads, group, count, *refs):
    sources, (blend, ids) = refs[:count], refs[count : count + 2]
    packed, (bias, sems, wide) = refs[-4 - group : -3], refs[-3:]
    message_rows = sum(source.shape[0] for source in sources)
    copies = start_block(sources, packed[0], partner(0, group) * heads, sems.at[0])
    for distance in range(group):
        kept = sources if distance < group // 2 else sources[1:]
        start = group * heads + lax.rem(partner(distance, group), group // 2) * 2
        copies += start_block(kept, packed[1 + distance], start, sems.at[1 + distance])
    bias[...] = jnp.where(ids[...] != 0, 0.0, -jnp.inf)
    store_weights(blend, wide, packed[0], message_rows)
    for copy in copies:
        copy.wait()


def prepare(sources, blend, ids, heads, group, after):
    rows = sum(source.shape[0] for source in sources)
    dtype = sources[0].dtype
    outs = [jax.ShapeDtypeStruct((rows + weight_rows(blend), heads * HEAD_DIM), dtype)]
    for distance in range(group):
        kept = rows if distance < group // 2 else rows - sources[0].shape[0]
        outs.append(jax.ShapeDtypeStruct((kept, 2 * HEAD_DIM), dtype))
    outs.append(jax.ShapeDtypeStruct(ids.shape, jnp.float32))
    return pl.pallas_call(
        functools.partial(prepare_kernel, heads, group, len(sources)),
        out_shape=outs,
        in_specs=[ANY] * len(sources) + [VMEM] * 2 + [ANY] * len(after),
        out_specs=[VMEM] * len(outs),
        scratch_shapes=[
            pltpu.SemaphoreType.DMA((len(outs), len(sources))),
            pltpu.VMEM(wide_shape(blend), jnp.float32),
        ],
        compiler_params=SMALL,
        cost_estimate=NO_COST,
        name="prepare",
    )(*sources, blend, ids, *after)


def attend_kernel(group, image_rows, text_rows, query_blocks, outputs, store, bias, *refs):
    blocks, outs, (keys, values) = refs[:group], refs[-2 - outputs : -2], refs[-2:]
    key_rows = image_rows + text_rows
    for distance in range(group):
        block = blocks[distance]
        source = partner(distance, group)
        image = pl.ds(distance * image_rows, image_rows)
        text = pl.ds(pl.multiple_of(group * image_rows + source * text_rows, text_rows), text_rows)
        key_at = image_rows if distance < query_blocks else 0
        value_at = key_at + key_rows
        keys[image] = block[key_at : key_at + image_rows]
        keys[text] = block[key_at + image_rows : key_at + key_rows]
        values[image] = block[value_at : value_at + image_rows]
        values[text] = block[value_at + image_rows : value_at + key_rows]
    image_keys = group * image_rows
    for at_head in range(0, keys.shape[1], HEAD_DIM):
        head = slice(at_head, at_head + HEAD_DIM)
        for distance in range(query_blocks):
            scores = lax.dot_general(
                blocks[distance][:image_rows, head],
                keys[:, head],
                (((1,), (1,)), ((), ())),
                preferred_element_type=jnp.float32,
            )
            scores = jnp.concatenate(
                [scores[:, :image_keys], scores[:, image_keys:] + bias[...]], axis=1
            )
            peak = jnp.max(scores, axis=1, keepdims=True)
            weights = jnp.exp2((scores - peak) * EXP2_SCALE)
            total = jnp.sum(weights, axis=1, keepdims=True)
            result = jnp.dot(
                weights.astype(jnp.bfloat16), values[:, head], preferred_element_type=jnp.float32
            )
            result = (result / total).astype(jnp.bfloat16)
            store(outs, result, distance, head)


def store_strips(outs, result, distance, head):
    rows = result.shape[0]
    for row in range(rows // WCOLS):
        at = distance * rows // 2 + row * STRIDE
        for side, out in enumerate(outs):
            start = row * WCOLS + side * STRIDE
            out[at : at + STRIDE, head] = result[start : start + STRIDE]


def store_blocks(outs, result, distance, head):
    rows = result.shape[0]
    both = outs[3 * distance]
    for row in range(rows // WCOLS):
        at = row * STRIDE
        for side, out in enumerate(outs[3 * distance + 1 : 3 * distance + 3]):
            start = row * WCOLS + side * STRIDE
            out[at : at + STRIDE, head] = result[start : start + STRIDE]
            at_both = at + side * rows // 2
            both[at_both : at_both + STRIDE, head] = result[start : start + STRIDE]


def attend(blocks, query_blocks, bias, image_rows, text_rows, store, after):
    group, width = len(blocks), blocks[0].shape[1]
    half = image_rows // 2
    if store is store_strips:
        rows = [query_blocks * half] * 2
    else:
        rows = [image_rows, half, half] * query_blocks
    keys = pltpu.VMEM((group * (image_rows + text_rows), width), jnp.bfloat16)
    return pl.pallas_call(
        functools.partial(
            attend_kernel, group, image_rows, text_rows, query_blocks, len(rows), store
        ),
        out_shape=[jax.ShapeDtypeStruct((count, width), jnp.bfloat16) for count in rows],
        in_specs=[VMEM] * (1 + group) + [ANY] * len(after),
        out_specs=[VMEM] * len(rows),
        scratch_shapes=[keys, keys],
        compiler_params=SMALL,
        cost_estimate=NO_COST,
        name="attend",
    )(bias, *blocks, *after)


def weigh_kernel(group, weight_row, image_rows, *refs):
    blocks, (weight_left, weight_right) = refs[:group], refs[group:]
    half = image_rows // 2
    for distance in range(group):
        columns = blocks[distance][weight_row : weight_row + 16, :128].astype(jnp.float32).T
        for row in range(image_rows // WCOLS):
            column, start = row * WCOLS // 128, row * WCOLS % 128
            at = distance * half + row * STRIDE
            for side, out in ((0, weight_left), (1, weight_right)):
                first = start + side * STRIDE
                out[at : at + STRIDE] = jnp.broadcast_to(
                    columns[first : first + STRIDE, column : column + 1], (STRIDE, HEAD_DIM)
                )


def weigh(blocks, weight_row, image_rows):
    group = len(blocks)
    out = jax.ShapeDtypeStruct((group * image_rows // 2, HEAD_DIM), jnp.float32)
    return pl.pallas_call(
        functools.partial(weigh_kernel, group, weight_row, image_rows),
        out_shape=[out, out],
        in_specs=[VMEM] * group,
        out_specs=[VMEM, VMEM],
        compiler_params=SMALL,
        cost_estimate=NO_COST,
        name="weigh",
    )(*blocks)


def mix(weight, own, other):
    mixed = weight * own.astype(jnp.float32) + (BLEND_TOTAL - weight) * other.astype(jnp.float32)
    return (mixed * (1.0 / BLEND_TOTAL)).astype(jnp.bfloat16)


def blend_kernel(own, other, weight, *outs):
    half = outs[0].shape[0]
    for distance, out in enumerate(outs):
        rows = pl.ds(distance * half, half)
        for at_head in range(0, own.shape[1], HEAD_DIM):
            head = pl.ds(at_head, HEAD_DIM)
            out[:, head] = mix(weight[rows], own[rows, head], other[rows, head])


def blend_strips(own, other, weight, blocks):
    rows, width = own.shape
    out = jax.ShapeDtypeStruct((rows // blocks, width), jnp.bfloat16)
    return pl.pallas_call(
        blend_kernel,
        out_shape=[out] * blocks,
        in_specs=[VMEM] * 3,
        out_specs=[VMEM] * blocks,
        compiler_params=SMALL,
        cost_estimate=NO_COST,
        name="blend",
    )(own, other, weight)


def load_kernel(w_out, *refs):
    out, sem = refs[-2:]
    copy = pltpu.make_async_copy(w_out, out, sem)
    copy.start()
    copy.wait()


def load_weights(w_out, after):
    return pl.pallas_call(
        load_kernel,
        out_shape=jax.ShapeDtypeStruct(w_out.shape, w_out.dtype),
        in_specs=[ANY] * (1 + len(after)),
        out_specs=VMEM,
        scratch_shapes=[pltpu.SemaphoreType.DMA],
        compiler_params=SMALL,
        cost_estimate=NO_COST,
        name="load_weights",
    )(w_out, *after)


def collect_kernel(group, *refs):
    blocks, out = refs[:group], refs[-1]
    width = blocks[0].shape[1]
    for distance in range(group):
        start = pl.multiple_of(partner(distance, group) * width, HEAD_DIM)
        out[:, pl.ds(start, width)] = blocks[distance][...]


def collect(blocks, after):
    group = len(blocks)
    rows, width = blocks[0].shape
    return pl.pallas_call(
        functools.partial(collect_kernel, group),
        out_shape=jax.ShapeDtypeStruct((rows, group * width), blocks[0].dtype),
        in_specs=[VMEM] * group + [ANY] * len(after),
        out_specs=VMEM,
        compiler_params=SMALL,
        cost_estimate=NO_COST,
        name="collect",
    )(*blocks, *after)


TILES = 6


def begin_kernel(left, right, weights, total, features):
    depth = features.shape[1]
    for row in range(features.shape[0] // WCOLS):
        strip = slice(row * STRIDE, (row + 1) * STRIDE)
        at = row * WCOLS
        features[at : at + STRIDE] = left[strip]
        features[at + STRIDE : at + WCOLS] = right[strip]
    tile = total.shape[1] // TILES
    for at in range(0, total.shape[1], tile):
        total[:, at : at + tile] = jnp.dot(
            features[...], weights[:depth, at : at + tile], preferred_element_type=jnp.float32
        )


def project_begin(left, right, weights):
    rows, depth = left.shape
    return pl.pallas_call(
        begin_kernel,
        out_shape=jax.ShapeDtypeStruct((2 * rows, weights.shape[1]), jnp.float32),
        in_specs=[VMEM] * 3,
        out_specs=VMEM,
        scratch_shapes=[pltpu.VMEM((2 * rows, depth), jnp.bfloat16)],
        compiler_params=SMALL,
        cost_estimate=NO_COST,
        name="project_begin",
    )(left, right, weights)


def end_kernel(group, *refs):
    blocks, refs = refs[:-8], refs[-8:]
    weight_left, weight_right, weights, total, out, features, result, sems = refs
    width, half = blocks[0].shape[1], features.shape[0] // 2
    for distance in range(len(blocks) // 3):
        own, from_prev, from_next = blocks[3 * distance : 3 * distance + 3]
        place = lax.rem(partner(distance, group), len(blocks) // 3)
        for at_head in range(0, width, HEAD_DIM):
            columns = pl.ds(pl.multiple_of(place * width + at_head, HEAD_DIM), HEAD_DIM)
            head = pl.ds(at_head, HEAD_DIM)
            for row in range(features.shape[0] // WCOLS):
                strip = pl.ds(row * STRIDE, STRIDE)
                for side, other, weight in (
                    (0, from_prev, weight_left),
                    (1, from_next, weight_right),
                ):
                    mine = own[pl.ds(side * half + row * STRIDE, STRIDE), head]
                    features[pl.ds(row * WCOLS + side * STRIDE, STRIDE), columns] = mix(
                        weight[strip], mine, other[strip, head]
                    )
    tile = result.shape[1] // TILES
    first = weights.shape[0] - features.shape[1]
    copies = []
    for at in range(0, result.shape[1], tile):
        columns = pl.ds(at, tile)
        product = jnp.dot(
            features[...], weights[first:, at : at + tile], preferred_element_type=jnp.float32
        )
        result[:, columns] = (total[:, columns] + product).astype(jnp.bfloat16)
        copy = pltpu.make_async_copy(
            result.at[:, columns], out.at[:, columns], sems.at[len(copies)]
        )
        copy.start()
        copies.append(copy)
    for copy in copies:
        copy.wait()


def project_end(blocks, weight_left, weight_right, weights, total, group):
    rows, width = total.shape
    depth = len(blocks) // 3 * blocks[0].shape[1]
    return pl.pallas_call(
        functools.partial(end_kernel, group),
        out_shape=jax.ShapeDtypeStruct((rows, width), jnp.bfloat16),
        in_specs=[VMEM] * (len(blocks) + 4),
        out_specs=ANY,
        scratch_shapes=[
            pltpu.VMEM((rows, depth), jnp.bfloat16),
            pltpu.VMEM((rows, width), jnp.bfloat16),
            pltpu.SemaphoreType.DMA((TILES,)),
        ],
        compiler_params=SMALL,
        cost_estimate=NO_COST,
        name="project_end",
    )(*blocks, weight_left, weight_right, weights, total)


def absorb(carried, keys, values, valid_keys, queries):
    running, denominator, numerator = carried
    scores = jnp.einsum("qhd,khd->qhk", queries, keys, preferred_element_type=jnp.float32) * SCALE
    scores = jnp.where(valid_keys[None, None, :], scores, -jnp.inf)
    updated = jnp.maximum(running, jnp.max(scores, axis=2))
    rescale = jnp.exp(running - updated)
    weights = jnp.exp(scores - updated[:, :, None])
    denominator = denominator * rescale + jnp.sum(weights, axis=2)
    product = jnp.einsum(
        "qhk,khd->qhd", weights.astype(jnp.bfloat16), values, preferred_element_type=jnp.float32
    )
    numerator = numerator * rescale[:, :, None] + product
    return (updated, denominator, numerator)


def attend_ring(blocks, query_blocks, prompt_ids, image_rows, text_rows, store):
    group, width = len(blocks), blocks[0].shape[1]
    head_count = width // HEAD_DIM
    key_rows = image_rows + text_rows
    queries = jnp.concatenate([block[:image_rows] for block in blocks[:query_blocks]], axis=0)
    starts = [image_rows if d < query_blocks else 0 for d in range(group)]
    keys, values = (
        jnp.concatenate(
            [block[at + s : at + s + key_rows] for block, s in zip(blocks, starts)], axis=0
        ).reshape(-1, head_count, HEAD_DIM)
        for at in (0, key_rows)
    )
    queries = queries.reshape(-1, head_count, HEAD_DIM)
    seq_count = lax.axis_size("seq")
    group_count = seq_count // group
    own_group = lax.axis_index("seq") // group
    order = (lax.axis_index("seq") % group) ^ jnp.arange(group)
    text_valid = prompt_ids.reshape(seq_count, text_rows) != 0

    def valid_for(source):
        text = lax.dynamic_slice_in_dim(text_valid, source * group, group, 0)[order]
        return jnp.concatenate([jnp.ones((group, image_rows), jnp.bool_), text], axis=1).reshape(-1)

    query_count = queries.shape[0]
    initial = (
        jnp.full((query_count, head_count), -jnp.inf, jnp.float32),
        jnp.zeros((query_count, head_count), jnp.float32),
        jnp.zeros((query_count, head_count, HEAD_DIM), jnp.float32),
    )
    carried = absorb(initial, keys, values, valid_for(own_group), queries)

    def one_turn(turn, state):
        current, keys, values = state
        keys, values = shifted(keys, "seq", group), shifted(values, "seq", group)
        source = (own_group - turn) % group_count
        return (absorb(current, keys, values, valid_for(source), queries), keys, values)

    carried, _, _ = lax.fori_loop(1, group_count, one_turn, (carried, keys, values))
    _, denominator, numerator = carried
    attended = (numerator / denominator[:, :, None]).astype(jnp.bfloat16)
    strips = [attended.reshape(-1, 2, STRIDE, width)[:, side] for side in range(2)]
    if store is store_strips:
        return [strip.reshape(-1, width) for strip in strips]
    sides = [strip.reshape(query_blocks, -1, width) for strip in strips]
    blocks = []
    for left, right in zip(*sides):
        blocks += [jnp.concatenate([left, right], axis=0), left, right]
    return blocks


def on_device(query, key_image, value_image, key_text, value_text, prompt_ids, blend, w_out):
    seq_count = lax.axis_size("seq")
    group = math.gcd(HEADS & -HEADS, seq_count)
    heads = HEADS // group - 1
    halfway = group // 2
    image_rows, text_rows = query.shape[1], key_text.shape[1]
    message_rows = 3 * image_rows + 2 * text_rows
    sources = [query[0], key_image[0], key_text[0], value_image[0], value_text[0]]

    far, near = tuple(range(halfway, group)), tuple(range(1, halfway))
    first = [None] * group
    for distances in (far, near):
        packed = pack(sources, blend, heads, group, distances)
        for distance, message in zip(distances, packed):
            first[distance] = swapped(message, distance)
    prepared = prepare(sources, blend, prompt_ids, heads, group, [first[halfway]])
    first[0], second, bias = prepared[0], prepared[1:-1], prepared[-1]
    second = [second[0]] + [swapped(second[d], d) for d in range(1, group)]
    weights = load_weights(w_out, [first[halfway]])
    weight_left, weight_right = weigh(first, message_rows, image_rows)

    if seq_count == group:
        def attended(blocks, query_blocks, store, after):
            return attend(blocks, query_blocks, bias, image_rows, text_rows, store, after)
    else:
        def attended(blocks, query_blocks, store, after):
            return attend_ring(
                blocks, query_blocks, prompt_ids[0], image_rows, text_rows, store
            )

    left, right = attended(first, group, store_strips, [])
    mixed = blend_strips(left, shifted(right, "win", 1), weight_left, group)
    begins = [mixed[0]] + [swapped(mixed[d], d) for d in range(1, group)]

    results = attended(second, halfway, store_blocks, [mixed[0], weights])
    blocks = []
    for distance in range(halfway):
        both, left, right = results[3 * distance : 3 * distance + 3]
        blocks += [
            swapped(both, distance) if distance else both,
            crossed(right, 1, distance),
            crossed(left, -1, distance),
        ]
    begins = collect(begins, [results[0]])
    total = project_begin(begins, shifted(begins, "win", -1), weights)
    return project_end(blocks, weight_left, weight_right, weights, total, group)[None]


def solution(mesh):
    tokens = P(("pano", "win"), "seq", None)
    return jax.shard_map(
        on_device,
        mesh=mesh,
        in_specs=(tokens,) * 5 + (P(("pano", "win"), None), P(("pano", "win"), "seq"), P()),
        out_specs=tokens,
        check_vma=False,
    )
```

```python
import functools
import math

import jax
import jax.numpy as jnp
from jax import lax
from jax.experimental import pallas as pl
from jax.experimental.pallas import tpu as pltpu
from jax.sharding import PartitionSpec as P

HEADS = 12
HEAD_DIM = 128
WCOLS = 64
STRIDE = 32
BLEND_TOTAL = 16.0
SCALE = HEAD_DIM ** (-0.5)
EXP2_SCALE = SCALE * math.log2(math.e)
MIB = 1024 * 1024
SMALL = pltpu.CompilerParams(vmem_limit_bytes=16 * MIB)
NO_COST = pl.CostEstimate(flops=0, bytes_accessed=0, transcendentals=0)
LARGE = pltpu.CompilerParams(vmem_limit_bytes=60 * MIB)

ANY = pl.BlockSpec(memory_space=pl.ANY)
VMEM = pl.BlockSpec(memory_space=pltpu.VMEM)


def shifted(block, axis, distance):
    count = lax.axis_size(axis)
    return lax.ppermute(block, axis, [(i, (i + distance) % count) for i in range(count)])


def swapped(block, distance):
    return lax.ppermute(block, "seq", [(i, i ^ distance) for i in range(lax.axis_size("seq"))])


def partner(distance, group):
    position = lax.rem(lax.axis_index("seq"), group)
    result, bit = 0, 1
    while bit < group:
        own = lax.rem(lax.div(position, bit), 2)
        result = result + (1 - own if distance & bit else own) * bit
        bit *= 2
    return result


def start_block(sources, packed, start, sems):
    columns = pl.ds(pl.multiple_of(start * HEAD_DIM, HEAD_DIM), packed.shape[1])
    copies, row = [], 0
    for source in sources:
        rows = source.shape[0]
        copy = pltpu.make_async_copy(
            source.at[:, columns], packed.at[pl.ds(row, rows)], sems.at[len(copies)]
        )
        copy.start()
        copies.append(copy)
        row += rows
    return copies


def store_weights(blend, wide, packed, row):
    wide[...] = jnp.zeros_like(wide)
    wide[:, : blend.shape[1]] = blend[...].astype(jnp.float32)
    rows, width = packed.shape[0] - row, packed.shape[1]
    index = lax.broadcasted_iota(jnp.int32, (rows, 128), 0)
    value = jnp.zeros((rows, 128), jnp.float32)
    for at in range(0, wide.shape[1], 128):
        value = jnp.where(index == at // 128, wide[:, at : at + 128], value)
    packed[row:, :128] = value.astype(packed.dtype)
    if width > 128:
        packed[row:, 128:] = jnp.zeros((rows, width - 128), packed.dtype)


def pack_kernel(heads, group, distances, count, *refs):
    sources, blend = refs[:count], refs[count]
    packed = refs[count + 1 : count + 1 + len(distances)]
    sems, blend_rows, wide = refs[count + 1 + len(distances) :]
    copies = []
    load = pltpu.make_async_copy(blend, blend_rows, sems.at[len(distances), 0])
    load.start()
    for index, distance in enumerate(distances):
        start = partner(distance, group) * heads
        copies += start_block(sources, packed[index], start, sems.at[index])
    load.wait()
    message_rows = sum(source.shape[0] for source in sources)
    for ref in packed:
        store_weights(blend_rows, wide, ref, message_rows)
    for copy in copies:
        copy.wait()


def weight_rows(blend):
    return -(-blend.shape[1] // (16 * 128)) * 16


def wide_shape(blend):
    return (1, -(-blend.shape[1] // 128) * 128)


def pack(sources, blend, heads, group, distances):
    rows = sum(source.shape[0] for source in sources) + weight_rows(blend)
    out = jax.ShapeDtypeStruct((rows, heads * HEAD_DIM), sources[0].dtype)
    return pl.pallas_call(
        functools.partial(pack_kernel, heads, group, distances, len(sources)),
        out_shape=[out] * len(distances),
        in_specs=[ANY] * (len(sources) + 1),
        out_specs=[VMEM] * len(distances),
        scratch_shapes=[
            pltpu.SemaphoreType.DMA((len(distances) + 1, len(sources))),
            pltpu.VMEM(blend.shape, blend.dtype),
            pltpu.VMEM(wide_shape(blend), jnp.float32),
        ],
        compiler_params=LARGE,
        cost_estimate=NO_COST,
        name="pack",
    )(*sources, blend)


def prepare_kernel(heads, group, count, *refs):
    sources, (blend, ids) = refs[:count], refs[count : count + 2]
    packed, (bias, sems, wide) = refs[-4 - group : -3], refs[-3:]
    message_rows = sum(source.shape[0] for source in sources)
    copies = start_block(sources, packed[0], partner(0, group) * heads, sems.at[0])
    for distance in range(group):
        kept = sources if distance < group // 2 else sources[1:]
        start = group * heads + lax.rem(partner(distance, group), group // 2) * 2
        copies += start_block(kept, packed[1 + distance], start, sems.at[1 + distance])
    bias[...] = jnp.where(ids[...] != 0, 0.0, -jnp.inf)
    store_weights(blend, wide, packed[0], message_rows)
    for copy in copies:
        copy.wait()


def prepare(sources, blend, ids, heads, group, after):
    rows = sum(source.shape[0] for source in sources)
    dtype = sources[0].dtype
    outs = [jax.ShapeDtypeStruct((rows + weight_rows(blend), heads * HEAD_DIM), dtype)]
    for distance in range(group):
        kept = rows if distance < group // 2 else rows - sources[0].shape[0]
        outs.append(jax.ShapeDtypeStruct((kept, 2 * HEAD_DIM), dtype))
    outs.append(jax.ShapeDtypeStruct(ids.shape, jnp.float32))
    return pl.pallas_call(
        functools.partial(prepare_kernel, heads, group, len(sources)),
        out_shape=outs,
        in_specs=[ANY] * len(sources) + [VMEM] * 2 + [ANY] * len(after),
        out_specs=[VMEM] * len(outs),
        scratch_shapes=[
            pltpu.SemaphoreType.DMA((len(outs), len(sources))),
            pltpu.VMEM(wide_shape(blend), jnp.float32),
        ],
        compiler_params=SMALL,
        cost_estimate=NO_COST,
        name="prepare",
    )(*sources, blend, ids, *after)


def soften(query, key, value, bias):
    scores = lax.dot_general(
        query, key, (((1,), (1,)), ((), ())), preferred_element_type=jnp.float32
    )
    image_keys = scores.shape[1] - bias.shape[1]
    scores = jnp.concatenate([scores[:, :image_keys], scores[:, image_keys:] + bias], axis=1)
    peak = jnp.max(scores, axis=1, keepdims=True)
    weights = jnp.exp2((scores - peak) * EXP2_SCALE)
    total = jnp.sum(weights, axis=1, keepdims=True)
    result = jnp.dot(weights.astype(jnp.bfloat16), value, preferred_element_type=jnp.float32)
    return (result / total).astype(jnp.bfloat16)


def half_kernel(group, image_rows, text_rows, bias, *refs):
    blocks, outs, (keys, values) = refs[:group], refs[-2 - group // 2 : -2], refs[-2:]
    key_rows = image_rows + text_rows
    for distance, block in enumerate(blocks):
        source = partner(distance, group)
        image = pl.ds(distance * image_rows, image_rows)
        text = pl.ds(pl.multiple_of(group * image_rows + source * text_rows, text_rows), text_rows)
        key_at = image_rows if distance < group // 2 else 0
        for ref, at in ((keys, key_at), (values, key_at + key_rows)):
            ref[image] = block[at : at + image_rows]
            ref[text] = block[at + image_rows : at + key_rows]
    for at in range(0, keys.shape[1], HEAD_DIM):
        head = slice(at, at + HEAD_DIM)
        for block, out in zip(blocks, outs):
            out[:, head] = soften(block[:image_rows, head], keys[:, head], values[:, head], bias[...])


def attend_half(blocks, bias, image_rows, text_rows, after):
    group, width = len(blocks), blocks[0].shape[1]
    keys = pltpu.VMEM((group * (image_rows + text_rows), width), jnp.bfloat16)
    return pl.pallas_call(
        functools.partial(half_kernel, group, image_rows, text_rows),
        out_shape=[jax.ShapeDtypeStruct((image_rows, width), jnp.bfloat16)] * (group // 2),
        in_specs=[VMEM] * (1 + group) + [ANY] * len(after),
        out_specs=[VMEM] * (group // 2),
        scratch_shapes=[keys, keys],
        compiler_params=SMALL,
        cost_estimate=NO_COST,
        name="attend_half",
    )(bias, *blocks, *after)


def merge_kernel(group, *refs):
    blocks, (left, right) = refs[: group // 2], refs[-2:]
    width = blocks[0].shape[1]
    for distance, block in enumerate(blocks):
        start = lax.rem(partner(distance, group), group // 2) * width
        columns = pl.ds(pl.multiple_of(start, HEAD_DIM), width)
        for row in range(block.shape[0] // WCOLS):
            for side, out in enumerate((left, right)):
                at = row * WCOLS + side * STRIDE
                out[pl.ds(row * STRIDE, STRIDE), columns] = block[at : at + STRIDE]


def merge(blocks, group, after):
    rows, width = blocks[0].shape
    strip = jax.ShapeDtypeStruct((rows // 2, len(blocks) * width), jnp.bfloat16)
    return pl.pallas_call(
        functools.partial(merge_kernel, group),
        out_shape=[strip, strip],
        in_specs=[VMEM] * len(blocks) + [ANY] * len(after),
        out_specs=[VMEM] * 2,
        compiler_params=SMALL,
        cost_estimate=NO_COST,
        name="merge",
    )(*blocks, *after)


def attend_kernel(group, image_rows, text_rows, bias, *refs):
    blocks, lefts, rights, (keys, values) = refs[:group], refs[-6:-4], refs[-4:-2], refs[-2:]
    key_rows = image_rows + text_rows
    for distance, block in enumerate(blocks):
        source = partner(distance, group)
        image = pl.ds(distance * image_rows, image_rows)
        text = pl.ds(pl.multiple_of(group * image_rows + source * text_rows, text_rows), text_rows)
        for ref, at in ((keys, image_rows), (values, image_rows + key_rows)):
            ref[image] = block[at : at + image_rows]
            ref[text] = block[at + image_rows : at + key_rows]
    half = image_rows // 2
    for at_head in range(0, keys.shape[1], HEAD_DIM):
        head = slice(at_head, at_head + HEAD_DIM)
        for distance, block in enumerate(blocks):
            result = soften(block[:image_rows, head], keys[:, head], values[:, head], bias[...])
            piece, place = divmod(distance, group // 2)
            left, right = lefts[piece], rights[piece]
            for row in range(image_rows // WCOLS):
                at = place * half + row * STRIDE
                left[at : at + STRIDE, head] = result[row * WCOLS : row * WCOLS + STRIDE]
                right[at : at + STRIDE, head] = result[row * WCOLS + STRIDE : (row + 1) * WCOLS]


def attend(blocks, bias, image_rows, text_rows):
    group, width = len(blocks), blocks[0].shape[1]
    strip = jax.ShapeDtypeStruct((group // 2 * image_rows // 2, width), jnp.bfloat16)
    keys = pltpu.VMEM((group * (image_rows + text_rows), width), jnp.bfloat16)
    strips = pl.pallas_call(
        functools.partial(attend_kernel, group, image_rows, text_rows),
        out_shape=[strip] * 4,
        in_specs=[VMEM] * (1 + group),
        out_specs=[VMEM] * 4,
        scratch_shapes=[keys, keys],
        compiler_params=SMALL,
        cost_estimate=NO_COST,
        name="attend",
    )(bias, *blocks)
    return strips[:2], strips[2:]


def weigh_kernel(group, weight_row, image_rows, *refs):
    blocks, outs = refs[:group], refs[group:]
    half = image_rows // 2
    for distance in range(group):
        columns = blocks[distance][weight_row : weight_row + 16, :128].astype(jnp.float32).T
        for row in range(image_rows // WCOLS):
            column, start = row * WCOLS // 128, row * WCOLS % 128
            piece, place = divmod(distance, group // 2)
            at = place * half + row * STRIDE
            for side, out in enumerate(outs[2 * piece : 2 * piece + 2]):
                first = start + side * STRIDE
                out[at : at + STRIDE] = jnp.broadcast_to(
                    columns[first : first + STRIDE, column : column + 1], (STRIDE, HEAD_DIM)
                )


def weigh(blocks, weight_row, image_rows):
    group = len(blocks)
    out = jax.ShapeDtypeStruct((group // 2 * image_rows // 2, HEAD_DIM), jnp.float32)
    return pl.pallas_call(
        functools.partial(weigh_kernel, group, weight_row, image_rows),
        out_shape=[out] * 4,
        in_specs=[VMEM] * group,
        out_specs=[VMEM] * 4,
        compiler_params=SMALL,
        cost_estimate=NO_COST,
        name="weigh",
    )(*blocks)


def blend_kernel(count, *refs):
    sides, outs = refs[: 3 * count], refs[3 * count :]
    half, blocks = outs[0].shape[0], len(outs) // count
    for index, out in enumerate(outs):
        own, other, weight_ref = sides[index // blocks * 3 : index // blocks * 3 + 3]
        rows = pl.ds(index % blocks * half, half)
        for at_head in range(0, own.shape[1], HEAD_DIM):
            head = pl.ds(at_head, HEAD_DIM)
            weight = weight_ref[rows]
            mixed = weight * own[rows, head].astype(jnp.float32)
            mixed += (BLEND_TOTAL - weight) * other[rows, head].astype(jnp.float32)
            out[:, head] = (mixed * (1.0 / BLEND_TOTAL)).astype(jnp.bfloat16)


def blend_strips(sides, blocks):
    rows, width = sides[0][0].shape
    out = jax.ShapeDtypeStruct((len(sides) * rows // blocks, width), jnp.bfloat16)
    return pl.pallas_call(
        functools.partial(blend_kernel, len(sides)),
        out_shape=[out] * blocks,
        in_specs=[VMEM] * (3 * len(sides)),
        out_specs=[VMEM] * blocks,
        compiler_params=SMALL,
        cost_estimate=NO_COST,
        name="blend",
    )(*sum(sides, ()))


def load_kernel(w_out, *refs):
    out, sem = refs[-2:]
    copy = pltpu.make_async_copy(w_out, out, sem)
    copy.start()
    copy.wait()


def load_weights(w_out, after):
    return pl.pallas_call(
        load_kernel,
        out_shape=jax.ShapeDtypeStruct(w_out.shape, w_out.dtype),
        in_specs=[ANY] * (1 + len(after)),
        out_specs=VMEM,
        scratch_shapes=[pltpu.SemaphoreType.DMA],
        compiler_params=SMALL,
        cost_estimate=NO_COST,
        name="load_weights",
    )(w_out, *after)


def hold_kernel(source, *refs):
    refs[-1][...] = source[...]


def hold(array, after):
    return pl.pallas_call(
        hold_kernel,
        out_shape=jax.ShapeDtypeStruct(array.shape, array.dtype),
        in_specs=[VMEM] + [ANY] * len(after),
        out_specs=VMEM,
        compiler_params=SMALL,
        cost_estimate=NO_COST,
        name="hold",
    )(array, *after)


def collect_kernel(group, *refs):
    blocks, out = refs[:group], refs[-1]
    width = blocks[0].shape[1]
    for distance in range(group):
        start = pl.multiple_of(partner(distance, group) * width, HEAD_DIM)
        out[:, pl.ds(start, width)] = blocks[distance][...]


def collect(blocks):
    group = len(blocks)
    rows, width = blocks[0].shape
    return pl.pallas_call(
        functools.partial(collect_kernel, group),
        out_shape=jax.ShapeDtypeStruct((rows, group * width), blocks[0].dtype),
        in_specs=[VMEM] * group,
        out_specs=VMEM,
        compiler_params=SMALL,
        cost_estimate=NO_COST,
        name="collect",
    )(*blocks)


TILES = 6


def begin_kernel(left, right, weights, total, features):
    depth = features.shape[1]
    for row in range(features.shape[0] // WCOLS):
        strip = slice(row * STRIDE, (row + 1) * STRIDE)
        at = row * WCOLS
        features[at : at + STRIDE] = left[strip]
        features[at + STRIDE : at + WCOLS] = right[strip]
    tile = total.shape[1] // TILES
    for at in range(0, total.shape[1], tile):
        total[:, at : at + tile] = jnp.dot(
            features[...], weights[:depth, at : at + tile], preferred_element_type=jnp.float32
        )


def project_begin(left, right, weights):
    rows, depth = left.shape
    return pl.pallas_call(
        begin_kernel,
        out_shape=jax.ShapeDtypeStruct((2 * rows, weights.shape[1]), jnp.float32),
        in_specs=[VMEM] * 3,
        out_specs=VMEM,
        scratch_shapes=[pltpu.VMEM((2 * rows, depth), jnp.bfloat16)],
        compiler_params=SMALL,
        cost_estimate=NO_COST,
        name="project_begin",
    )(left, right, weights)


def end_kernel(left, right, from_prev, from_next, *refs):
    weight_left, weight_right, weights, total, out, features, result, sems = refs
    rows = left.shape[0]
    for side, (own, other, weight_ref) in enumerate(
        ((left, from_prev, weight_left), (right, from_next, weight_right))
    ):
        weight = weight_ref[:rows]
        for at in range(0, own.shape[1], HEAD_DIM):
            head = pl.ds(at, HEAD_DIM)
            mixed = weight * own[:, head].astype(jnp.float32)
            mixed += (BLEND_TOTAL - weight) * other[:, head].astype(jnp.float32)
            mixed = (mixed * (1.0 / BLEND_TOTAL)).astype(jnp.bfloat16)
            for row in range(rows // STRIDE):
                start = row * WCOLS + side * STRIDE
                features[pl.ds(start, STRIDE), head] = mixed[row * STRIDE : (row + 1) * STRIDE]
    tile = result.shape[1] // TILES
    first = weights.shape[0] - features.shape[1]
    copies = []
    for at in range(0, result.shape[1], tile):
        columns = pl.ds(at, tile)
        product = jnp.dot(
            features[...], weights[first:, at : at + tile], preferred_element_type=jnp.float32
        )
        result[:, columns] = (total[:, columns] + product).astype(jnp.bfloat16)
        copy = pltpu.make_async_copy(
            result.at[:, columns], out.at[:, columns], sems.at[len(copies)]
        )
        copy.start()
        copies.append(copy)
    for copy in copies:
        copy.wait()


def project_end(strips, blend_weights, weights, total):
    rows, width = total.shape
    return pl.pallas_call(
        end_kernel,
        out_shape=jax.ShapeDtypeStruct((rows, width), jnp.bfloat16),
        in_specs=[VMEM] * 8,
        out_specs=ANY,
        scratch_shapes=[
            pltpu.VMEM((rows, strips[0].shape[1]), jnp.bfloat16),
            pltpu.VMEM((rows, width), jnp.bfloat16),
            pltpu.SemaphoreType.DMA((TILES,)),
        ],
        compiler_params=SMALL,
        cost_estimate=NO_COST,
        name="project_end",
    )(*strips, *blend_weights, weights, total)


def absorb(carried, keys, values, valid_keys, queries):
    running, denominator, numerator = carried
    scores = jnp.einsum("qhd,khd->qhk", queries, keys, preferred_element_type=jnp.float32) * SCALE
    scores = jnp.where(valid_keys[None, None, :], scores, -jnp.inf)
    updated = jnp.maximum(running, jnp.max(scores, axis=2))
    rescale = jnp.exp(running - updated)
    weights = jnp.exp(scores - updated[:, :, None])
    denominator = denominator * rescale + jnp.sum(weights, axis=2)
    product = jnp.einsum(
        "qhk,khd->qhd", weights.astype(jnp.bfloat16), values, preferred_element_type=jnp.float32
    )
    numerator = numerator * rescale[:, :, None] + product
    return (updated, denominator, numerator)


def attend_ring(blocks, query_blocks, prompt_ids, image_rows, text_rows):
    group, width = len(blocks), blocks[0].shape[1]
    head_count = width // HEAD_DIM
    key_rows = image_rows + text_rows
    queries = jnp.concatenate([block[:image_rows] for block in blocks[:query_blocks]], axis=0)
    starts = [image_rows if d < query_blocks else 0 for d in range(group)]
    keys, values = (
        jnp.concatenate(
            [block[at + s : at + s + key_rows] for block, s in zip(blocks, starts)], axis=0
        ).reshape(-1, head_count, HEAD_DIM)
        for at in (0, key_rows)
    )
    queries = queries.reshape(-1, head_count, HEAD_DIM)
    seq_count = lax.axis_size("seq")
    group_count = seq_count // group
    own_group = lax.axis_index("seq") // group
    order = (lax.axis_index("seq") % group) ^ jnp.arange(group)
    text_valid = prompt_ids.reshape(seq_count, text_rows) != 0

    def valid_for(source):
        text = lax.dynamic_slice_in_dim(text_valid, source * group, group, 0)[order]
        return jnp.concatenate([jnp.ones((group, image_rows), jnp.bool_), text], axis=1).reshape(-1)

    query_count = queries.shape[0]
    initial = (
        jnp.full((query_count, head_count), -jnp.inf, jnp.float32),
        jnp.zeros((query_count, head_count), jnp.float32),
        jnp.zeros((query_count, head_count, HEAD_DIM), jnp.float32),
    )
    carried = absorb(initial, keys, values, valid_for(own_group), queries)

    def one_turn(turn, state):
        current, keys, values = state
        keys, values = shifted(keys, "seq", group), shifted(values, "seq", group)
        source = (own_group - turn) % group_count
        return (absorb(current, keys, values, valid_for(source), queries), keys, values)

    carried, _, _ = lax.fori_loop(1, group_count, one_turn, (carried, keys, values))
    _, denominator, numerator = carried
    attended = (numerator / denominator[:, :, None]).astype(jnp.bfloat16)
    return attended.reshape(query_blocks, image_rows, width)


def ring_strips(blocks, prompt_ids, image_rows, text_rows):
    group = len(blocks)
    attended = attend_ring(blocks, group, prompt_ids, image_rows, text_rows)
    sides = attended.reshape(2, -1, 2, STRIDE, attended.shape[2])
    return [[sides[p, :, s].reshape(-1, attended.shape[2]) for p in range(2)] for s in range(2)]


def ring_half(blocks, prompt_ids, image_rows, text_rows):
    return list(attend_ring(blocks, len(blocks) // 2, prompt_ids, image_rows, text_rows))


def on_device(query, key_image, value_image, key_text, value_text, prompt_ids, blend, w_out):
    seq_count = lax.axis_size("seq")
    group = math.gcd(HEADS & -HEADS, seq_count)
    heads = HEADS // group - 1
    halfway = group // 2
    image_rows, text_rows = query.shape[1], key_text.shape[1]
    message_rows = 3 * image_rows + 2 * text_rows
    sources = [query[0], key_image[0], key_text[0], value_image[0], value_text[0]]

    far, near = tuple(range(halfway, group)), tuple(range(1, halfway))
    received = [None] * group
    for distances in (far, near):
        packed = pack(sources, blend, heads, group, distances)
        for distance, message in zip(distances, packed):
            received[distance] = swapped(message, distance)
    weights = load_weights(w_out, [])
    prepared = prepare(sources, blend, prompt_ids, heads, group, [weights])
    received[0], packed, bias = prepared[0], prepared[1:-1], prepared[-1]
    first = received
    second = [packed[0]] + [swapped(packed[d], d) for d in near]
    for distance in far:
        second.append(swapped(hold(packed[distance], first[halfway:]), distance))
    blend_weights = weigh(first, message_rows, image_rows)

    def strips_of(blocks):
        if seq_count == group:
            return attend(blocks, bias, image_rows, text_rows)
        return ring_strips(blocks, prompt_ids[0], image_rows, text_rows)

    def results_of(blocks, after):
        if seq_count == group:
            return attend_half(blocks, bias, image_rows, text_rows, after)
        return ring_half(blocks, prompt_ids[0], image_rows, text_rows)

    def returned(mixed):
        return [mixed[0]] + [swapped(mixed[d], d) for d in range(1, len(mixed))]

    lefts, rights = strips_of(first)
    sides = [
        (left, shifted(right, "win", 1), weight)
        for left, right, weight in zip(lefts, rights, blend_weights[::2])
    ]
    mixed = blend_strips(sides, group)
    begun = returned(mixed)

    results = returned(results_of(second, [mixed[0], weights]))
    left, right = merge(results, group, begun[1:])
    from_prev, from_next = shifted(right, "win", 1), shifted(left, "win", -1)
    begins = collect(begun)
    total = project_begin(begins, shifted(begins, "win", -1), weights)
    strips = [left, right, from_prev, from_next]
    return project_end(strips, blend_weights[:2], weights, total)[None]


def solution(mesh):
    tokens = P(("pano", "win"), "seq", None)
    return jax.shard_map(
        on_device,
        mesh=mesh,
        in_specs=(tokens,) * 5 + (P(("pano", "win"), None), P(("pano", "win"), "seq"), P()),
        out_specs=tokens,
        check_vma=False,
    )
```

```python
import functools
import math

import jax
import jax.numpy as jnp
from jax import lax
from jax.experimental import pallas as pl
from jax.experimental.pallas import tpu as pltpu
from jax.sharding import PartitionSpec as P

HEADS = 12
HEAD_DIM = 128
WCOLS = 64
STRIDE = 32
BLEND_TOTAL = 16.0
SCALE = HEAD_DIM ** (-0.5)
EXP2_SCALE = SCALE * math.log2(math.e)
MIB = 1024 * 1024
SMALL = pltpu.CompilerParams(vmem_limit_bytes=16 * MIB)
NO_COST = pl.CostEstimate(flops=0, bytes_accessed=0, transcendentals=0)
LARGE = pltpu.CompilerParams(vmem_limit_bytes=60 * MIB)

ANY = pl.BlockSpec(memory_space=pl.ANY)
VMEM = pl.BlockSpec(memory_space=pltpu.VMEM)


def shifted(block, axis, distance):
    count = lax.axis_size(axis)
    return lax.ppermute(block, axis, [(i, (i + distance) % count) for i in range(count)])


def swapped(block, distance):
    return lax.ppermute(block, "seq", [(i, i ^ distance) for i in range(lax.axis_size("seq"))])


def partner(distance, group):
    position = lax.rem(lax.axis_index("seq"), group)
    result, bit = 0, 1
    while bit < group:
        own = lax.rem(lax.div(position, bit), 2)
        result = result + (1 - own if distance & bit else own) * bit
        bit *= 2
    return result


def start_block(sources, packed, start, sems):
    columns = pl.ds(pl.multiple_of(start * HEAD_DIM, HEAD_DIM), packed.shape[1])
    copies, row = [], 0
    for source in sources:
        rows = source.shape[0]
        copy = pltpu.make_async_copy(
            source.at[:, columns], packed.at[pl.ds(row, rows)], sems.at[len(copies)]
        )
        copy.start()
        copies.append(copy)
        row += rows
    return copies


def store_weights(blend, wide, packed, row):
    wide[...] = jnp.zeros_like(wide)
    wide[:, : blend.shape[1]] = blend[...].astype(jnp.float32)
    rows, width = packed.shape[0] - row, packed.shape[1]
    index = lax.broadcasted_iota(jnp.int32, (rows, 128), 0)
    value = jnp.zeros((rows, 128), jnp.float32)
    for at in range(0, wide.shape[1], 128):
        value = jnp.where(index == at // 128, wide[:, at : at + 128], value)
    packed[row:, :128] = value.astype(packed.dtype)
    if width > 128:
        packed[row:, 128:] = jnp.zeros((rows, width - 128), packed.dtype)


def pack_kernel(heads, group, distances, count, *refs):
    sources, blend = refs[:count], refs[count]
    packed = refs[count + 1 : count + 1 + len(distances)]
    sems, blend_rows, wide = refs[count + 1 + len(distances) :]
    copies = []
    load = pltpu.make_async_copy(blend, blend_rows, sems.at[len(distances), 0])
    load.start()
    for index, distance in enumerate(distances):
        start = partner(distance, group) * heads
        copies += start_block(sources, packed[index], start, sems.at[index])
    load.wait()
    message_rows = sum(source.shape[0] for source in sources)
    for ref in packed:
        store_weights(blend_rows, wide, ref, message_rows)
    for copy in copies:
        copy.wait()


def weight_rows(blend):
    return -(-blend.shape[1] // (16 * 128)) * 16


def wide_shape(blend):
    return (1, -(-blend.shape[1] // 128) * 128)


def pack(sources, blend, heads, group, distances):
    rows = sum(source.shape[0] for source in sources) + weight_rows(blend)
    out = jax.ShapeDtypeStruct((rows, heads * HEAD_DIM), sources[0].dtype)
    return pl.pallas_call(
        functools.partial(pack_kernel, heads, group, distances, len(sources)),
        out_shape=[out] * len(distances),
        in_specs=[ANY] * (len(sources) + 1),
        out_specs=[VMEM] * len(distances),
        scratch_shapes=[
            pltpu.SemaphoreType.DMA((len(distances) + 1, len(sources))),
            pltpu.VMEM(blend.shape, blend.dtype),
            pltpu.VMEM(wide_shape(blend), jnp.float32),
        ],
        compiler_params=SMALL,
        cost_estimate=NO_COST,
        name="pack",
    )(*sources, blend)


def prepare_kernel(heads, group, count, *refs):
    sources, (blend, ids) = refs[:count], refs[count : count + 2]
    packed, (bias, sems, wide) = refs[-4 - group : -3], refs[-3:]
    message_rows = sum(source.shape[0] for source in sources)
    copies = start_block(sources, packed[0], partner(0, group) * heads, sems.at[0])
    for distance in range(group):
        kept = sources if distance < group // 2 else sources[1:]
        start = group * heads + lax.rem(partner(distance, group), group // 2) * 2
        copies += start_block(kept, packed[1 + distance], start, sems.at[1 + distance])
    bias[...] = jnp.where(ids[...] != 0, 0.0, -jnp.inf)
    store_weights(blend, wide, packed[0], message_rows)
    for copy in copies:
        copy.wait()


def prepare(sources, blend, ids, heads, group, after):
    rows = sum(source.shape[0] for source in sources)
    dtype = sources[0].dtype
    outs = [jax.ShapeDtypeStruct((rows + weight_rows(blend), heads * HEAD_DIM), dtype)]
    for distance in range(group):
        kept = rows if distance < group // 2 else rows - sources[0].shape[0]
        outs.append(jax.ShapeDtypeStruct((kept, 2 * HEAD_DIM), dtype))
    outs.append(jax.ShapeDtypeStruct(ids.shape, jnp.float32))
    return pl.pallas_call(
        functools.partial(prepare_kernel, heads, group, len(sources)),
        out_shape=outs,
        in_specs=[ANY] * len(sources) + [VMEM] * 2 + [ANY] * len(after),
        out_specs=[VMEM] * len(outs),
        scratch_shapes=[
            pltpu.SemaphoreType.DMA((len(outs), len(sources))),
            pltpu.VMEM(wide_shape(blend), jnp.float32),
        ],
        compiler_params=SMALL,
        cost_estimate=NO_COST,
        name="prepare",
    )(*sources, blend, ids, *after)


def soften(query, key, value, bias):
    scores = lax.dot_general(
        query, key, (((1,), (1,)), ((), ())), preferred_element_type=jnp.float32
    )
    image_keys = scores.shape[1] - bias.shape[1]
    scores = jnp.concatenate([scores[:, :image_keys], scores[:, image_keys:] + bias], axis=1)
    peak = jnp.max(scores, axis=1, keepdims=True)
    weights = jnp.exp2((scores - peak) * EXP2_SCALE)
    total = jnp.sum(weights, axis=1, keepdims=True)
    result = jnp.dot(weights.astype(jnp.bfloat16), value, preferred_element_type=jnp.float32)
    return (result / total).astype(jnp.bfloat16)


def fill(keys, values, mask, bias, blocks, sources, starts, group, image_rows, text_rows):
    key_rows, texts = image_rows + text_rows, group * text_rows
    for ref, offset in ((keys, 0), (values, key_rows)):
        ref[:texts] = jnp.zeros((texts, ref.shape[1]), ref.dtype)
        for index, (block, source, start) in enumerate(zip(blocks, sources, starts)):
            at, image = start + offset, texts + index * image_rows
            ref[image : image + image_rows] = block[at : at + image_rows]
            text = pl.ds(pl.multiple_of(source * text_rows, text_rows), text_rows)
            ref[text] = block[at + image_rows : at + key_rows]
    lane = lax.broadcasted_iota(jnp.int32, bias.shape, 1)
    here = jnp.zeros(bias.shape, jnp.int32)
    for source in sources:
        inside = (lane >= source * text_rows) & (lane < (source + 1) * text_rows)
        here = jnp.where(inside, 1, here)
    mask[...] = jnp.zeros_like(mask)
    mask[:, :texts] = jnp.where(here == 1, bias[...], -jnp.inf)


def sum_up(query, key, value, mask, peak=None):
    scores = lax.dot_general(
        query, key, (((1,), (1,)), ((), ())), preferred_element_type=jnp.float32
    )
    scores = scores + mask
    highest = jnp.max(scores, axis=1, keepdims=True)
    highest = jnp.broadcast_to(highest, (scores.shape[0], HEAD_DIM))
    if peak is not None:
        highest = jnp.maximum(highest, peak)
    tiles = -(-scores.shape[1] // HEAD_DIM)
    wide = jnp.concatenate([highest] * tiles, axis=1)[:, : scores.shape[1]]
    weights = jnp.exp2((scores - wide) * EXP2_SCALE)
    total = jnp.broadcast_to(jnp.sum(weights, axis=1, keepdims=True), highest.shape)
    product = jnp.dot(weights.astype(jnp.bfloat16), value, preferred_element_type=jnp.float32)
    return product, total, highest


def early_kernel(group, image_rows, text_rows, bias, *refs):
    halfway = group // 2
    blocks = refs[: group - 1]
    products, totals, peaks, keys, values, mask = refs[-6:]
    distances = [d for d in range(group) if d != halfway]
    sources = [partner(d, group) for d in distances]
    starts = [image_rows if d < halfway else 0 for d in distances]
    fill(keys, values, mask, bias, blocks, sources, starts, group, image_rows, text_rows)
    for at in range(0, keys.shape[1], HEAD_DIM):
        head = slice(at, at + HEAD_DIM)
        for index in range(halfway):
            rows = slice(index * image_rows, (index + 1) * image_rows)
            product, total, peak = sum_up(
                blocks[index][:image_rows, head],
                keys[:, head],
                values[:, head],
                mask[...],
            )
            products[rows, head] = product
            totals[rows, head] = total
            peaks[rows, head] = peak


def late_kernel(group, image_rows, text_rows, bias, products, totals, peaks, *refs):
    halfway = group // 2
    near, block = refs[:halfway], refs[halfway]
    outs, (keys, values, mask) = refs[-3 - halfway : -3], refs[-3:]
    sources = [partner(halfway, group)]
    fill(keys, values, mask, bias, [block], sources, [0], group, image_rows, text_rows)
    for at in range(0, keys.shape[1], HEAD_DIM):
        head = slice(at, at + HEAD_DIM)
        for index, out in enumerate(outs):
            rows = slice(index * image_rows, (index + 1) * image_rows)
            before = peaks[rows, head]
            product, total, peak = sum_up(
                near[index][:image_rows, head],
                keys[:, head],
                values[:, head],
                mask[...],
                before,
            )
            scale = jnp.exp2((before - peak) * EXP2_SCALE)
            total += totals[rows, head] * scale
            product += products[rows, head] * scale
            out[:, head] = (product / total).astype(jnp.bfloat16)


def attend_half(blocks, bias, image_rows, text_rows, after):
    group, width = len(blocks), blocks[0].shape[1]
    halfway = group // 2
    near, last = list(blocks[:halfway]), blocks[halfway]
    others = near + list(blocks[halfway + 1 :])
    texts = group * text_rows
    total = jax.ShapeDtypeStruct((halfway * image_rows, width), jnp.float32)
    count = len(others) * image_rows + texts
    keys, mask = pltpu.VMEM((count, width), jnp.bfloat16), pltpu.VMEM((1, count), jnp.float32)
    sums = pl.pallas_call(
        functools.partial(early_kernel, group, image_rows, text_rows),
        out_shape=[total] * 3,
        in_specs=[VMEM] * group + [ANY] * len(after),
        out_specs=[VMEM] * 3,
        scratch_shapes=[keys, keys, mask],
        compiler_params=SMALL,
        cost_estimate=NO_COST,
        name="attend_early",
    )(bias, *others, *after)
    count = image_rows + texts
    keys, mask = pltpu.VMEM((count, width), jnp.bfloat16), pltpu.VMEM((1, count), jnp.float32)
    return pl.pallas_call(
        functools.partial(late_kernel, group, image_rows, text_rows),
        out_shape=[jax.ShapeDtypeStruct((image_rows, width), jnp.bfloat16)] * halfway,
        in_specs=[VMEM] * (5 + halfway),
        out_specs=[VMEM] * halfway,
        scratch_shapes=[keys, keys, mask],
        compiler_params=SMALL,
        cost_estimate=NO_COST,
        name="attend_late",
    )(bias, *sums, *near, last)


def merge_kernel(group, *refs):
    blocks, (left, right) = refs[: group // 2], refs[-2:]
    width = blocks[0].shape[1]
    for distance, block in enumerate(blocks):
        start = lax.rem(partner(distance, group), group // 2) * width
        columns = pl.ds(pl.multiple_of(start, HEAD_DIM), width)
        for row in range(block.shape[0] // WCOLS):
            for side, out in enumerate((left, right)):
                at = row * WCOLS + side * STRIDE
                out[pl.ds(row * STRIDE, STRIDE), columns] = block[at : at + STRIDE]


def merge(blocks, group, after):
    rows, width = blocks[0].shape
    strip = jax.ShapeDtypeStruct((rows // 2, len(blocks) * width), jnp.bfloat16)
    return pl.pallas_call(
        functools.partial(merge_kernel, group),
        out_shape=[strip, strip],
        in_specs=[VMEM] * len(blocks) + [ANY] * len(after),
        out_specs=[VMEM] * 2,
        compiler_params=SMALL,
        cost_estimate=NO_COST,
        name="merge",
    )(*blocks, *after)


def attend_kernel(group, image_rows, text_rows, bias, *refs):
    blocks, lefts, rights, (keys, values) = refs[:group], refs[-6:-4], refs[-4:-2], refs[-2:]
    key_rows = image_rows + text_rows
    for distance, block in enumerate(blocks):
        source = partner(distance, group)
        image = pl.ds(distance * image_rows, image_rows)
        text = pl.ds(pl.multiple_of(group * image_rows + source * text_rows, text_rows), text_rows)
        for ref, at in ((keys, image_rows), (values, image_rows + key_rows)):
            ref[image] = block[at : at + image_rows]
            ref[text] = block[at + image_rows : at + key_rows]
    half = image_rows // 2
    for at_head in range(0, keys.shape[1], HEAD_DIM):
        head = slice(at_head, at_head + HEAD_DIM)
        for distance, block in enumerate(blocks):
            result = soften(block[:image_rows, head], keys[:, head], values[:, head], bias[...])
            piece, place = divmod(distance, group // 2)
            left, right = lefts[piece], rights[piece]
            for row in range(image_rows // WCOLS):
                at = place * half + row * STRIDE
                left[at : at + STRIDE, head] = result[row * WCOLS : row * WCOLS + STRIDE]
                right[at : at + STRIDE, head] = result[row * WCOLS + STRIDE : (row + 1) * WCOLS]


def attend(blocks, bias, image_rows, text_rows):
    group, width = len(blocks), blocks[0].shape[1]
    strip = jax.ShapeDtypeStruct((group // 2 * image_rows // 2, width), jnp.bfloat16)
    keys = pltpu.VMEM((group * (image_rows + text_rows), width), jnp.bfloat16)
    strips = pl.pallas_call(
        functools.partial(attend_kernel, group, image_rows, text_rows),
        out_shape=[strip] * 4,
        in_specs=[VMEM] * (1 + group),
        out_specs=[VMEM] * 4,
        scratch_shapes=[keys, keys],
        compiler_params=SMALL,
        cost_estimate=NO_COST,
        name="attend",
    )(bias, *blocks)
    return strips[:2], strips[2:]


def weigh_kernel(group, weight_row, image_rows, *refs):
    blocks, outs = refs[:group], refs[group:]
    half = image_rows // 2
    for distance in range(group):
        columns = blocks[distance][weight_row : weight_row + 16, :128].astype(jnp.float32).T
        for row in range(image_rows // WCOLS):
            column, start = row * WCOLS // 128, row * WCOLS % 128
            piece, place = divmod(distance, group // 2)
            at = place * half + row * STRIDE
            for side, out in enumerate(outs[2 * piece : 2 * piece + 2]):
                first = start + side * STRIDE
                out[at : at + STRIDE] = jnp.broadcast_to(
                    columns[first : first + STRIDE, column : column + 1], (STRIDE, HEAD_DIM)
                )


def weigh(blocks, weight_row, image_rows):
    group = len(blocks)
    out = jax.ShapeDtypeStruct((group // 2 * image_rows // 2, HEAD_DIM), jnp.float32)
    return pl.pallas_call(
        functools.partial(weigh_kernel, group, weight_row, image_rows),
        out_shape=[out] * 4,
        in_specs=[VMEM] * group,
        out_specs=[VMEM] * 4,
        compiler_params=SMALL,
        cost_estimate=NO_COST,
        name="weigh",
    )(*blocks)


def blend_kernel(count, *refs):
    sides, outs = refs[: 3 * count], refs[3 * count :]
    half, blocks = outs[0].shape[0], len(outs) // count
    for index, out in enumerate(outs):
        own, other, weight_ref = sides[index // blocks * 3 : index // blocks * 3 + 3]
        rows = pl.ds(index % blocks * half, half)
        for at_head in range(0, own.shape[1], HEAD_DIM):
            head = pl.ds(at_head, HEAD_DIM)
            weight = weight_ref[rows]
            mixed = weight * own[rows, head].astype(jnp.float32)
            mixed += (BLEND_TOTAL - weight) * other[rows, head].astype(jnp.float32)
            out[:, head] = (mixed * (1.0 / BLEND_TOTAL)).astype(jnp.bfloat16)


def blend_strips(sides, blocks):
    rows, width = sides[0][0].shape
    out = jax.ShapeDtypeStruct((len(sides) * rows // blocks, width), jnp.bfloat16)
    return pl.pallas_call(
        functools.partial(blend_kernel, len(sides)),
        out_shape=[out] * blocks,
        in_specs=[VMEM] * (3 * len(sides)),
        out_specs=[VMEM] * blocks,
        compiler_params=SMALL,
        cost_estimate=NO_COST,
        name="blend",
    )(*sum(sides, ()))


def load_kernel(w_out, *refs):
    out, sem = refs[-2:]
    copy = pltpu.make_async_copy(w_out, out, sem)
    copy.start()
    copy.wait()


def load_weights(w_out, after):
    return pl.pallas_call(
        load_kernel,
        out_shape=jax.ShapeDtypeStruct(w_out.shape, w_out.dtype),
        in_specs=[ANY] * (1 + len(after)),
        out_specs=VMEM,
        scratch_shapes=[pltpu.SemaphoreType.DMA],
        compiler_params=SMALL,
        cost_estimate=NO_COST,
        name="load_weights",
    )(w_out, *after)


def hold_kernel(source, *refs):
    refs[-1][...] = source[...]


def hold(array, after):
    return pl.pallas_call(
        hold_kernel,
        out_shape=jax.ShapeDtypeStruct(array.shape, array.dtype),
        in_specs=[VMEM] + [ANY] * len(after),
        out_specs=VMEM,
        compiler_params=SMALL,
        cost_estimate=NO_COST,
        name="hold",
    )(array, *after)


def collect_kernel(group, *refs):
    blocks, out = refs[:group], refs[-1]
    width = blocks[0].shape[1]
    for distance in range(group):
        start = pl.multiple_of(partner(distance, group) * width, HEAD_DIM)
        out[:, pl.ds(start, width)] = blocks[distance][...]


def collect(blocks):
    group = len(blocks)
    rows, width = blocks[0].shape
    return pl.pallas_call(
        functools.partial(collect_kernel, group),
        out_shape=jax.ShapeDtypeStruct((rows, group * width), blocks[0].dtype),
        in_specs=[VMEM] * group,
        out_specs=VMEM,
        compiler_params=SMALL,
        cost_estimate=NO_COST,
        name="collect",
    )(*blocks)


TILES = 6


def begin_kernel(left, right, weights, total, features):
    depth = features.shape[1]
    for row in range(features.shape[0] // WCOLS):
        strip = slice(row * STRIDE, (row + 1) * STRIDE)
        at = row * WCOLS
        features[at : at + STRIDE] = left[strip]
        features[at + STRIDE : at + WCOLS] = right[strip]
    tile = total.shape[1] // TILES
    for at in range(0, total.shape[1], tile):
        total[:, at : at + tile] = jnp.dot(
            features[...], weights[:depth, at : at + tile], preferred_element_type=jnp.float32
        )


def project_begin(left, right, weights):
    rows, depth = left.shape
    return pl.pallas_call(
        begin_kernel,
        out_shape=jax.ShapeDtypeStruct((2 * rows, weights.shape[1]), jnp.float32),
        in_specs=[VMEM] * 3,
        out_specs=VMEM,
        scratch_shapes=[pltpu.VMEM((2 * rows, depth), jnp.bfloat16)],
        compiler_params=SMALL,
        cost_estimate=NO_COST,
        name="project_begin",
    )(left, right, weights)


def end_kernel(left, right, from_prev, from_next, *refs):
    weight_left, weight_right, weights, total, out, features, result, sems = refs
    rows = left.shape[0]
    for side, (own, other, weight_ref) in enumerate(
        ((left, from_prev, weight_left), (right, from_next, weight_right))
    ):
        weight = weight_ref[:rows]
        for at in range(0, own.shape[1], HEAD_DIM):
            head = pl.ds(at, HEAD_DIM)
            mixed = weight * own[:, head].astype(jnp.float32)
            mixed += (BLEND_TOTAL - weight) * other[:, head].astype(jnp.float32)
            mixed = (mixed * (1.0 / BLEND_TOTAL)).astype(jnp.bfloat16)
            for row in range(rows // STRIDE):
                start = row * WCOLS + side * STRIDE
                features[pl.ds(start, STRIDE), head] = mixed[row * STRIDE : (row + 1) * STRIDE]
    tile = result.shape[1] // TILES
    first = weights.shape[0] - features.shape[1]
    copies = []
    for at in range(0, result.shape[1], tile):
        columns = pl.ds(at, tile)
        product = jnp.dot(
            features[...], weights[first:, at : at + tile], preferred_element_type=jnp.float32
        )
        result[:, columns] = (total[:, columns] + product).astype(jnp.bfloat16)
        copy = pltpu.make_async_copy(
            result.at[:, columns], out.at[:, columns], sems.at[len(copies)]
        )
        copy.start()
        copies.append(copy)
    for copy in copies:
        copy.wait()


def project_end(strips, blend_weights, weights, total):
    rows, width = total.shape
    return pl.pallas_call(
        end_kernel,
        out_shape=jax.ShapeDtypeStruct((rows, width), jnp.bfloat16),
        in_specs=[VMEM] * 8,
        out_specs=ANY,
        scratch_shapes=[
            pltpu.VMEM((rows, strips[0].shape[1]), jnp.bfloat16),
            pltpu.VMEM((rows, width), jnp.bfloat16),
            pltpu.SemaphoreType.DMA((TILES,)),
        ],
        compiler_params=SMALL,
        cost_estimate=NO_COST,
        name="project_end",
    )(*strips, *blend_weights, weights, total)


def absorb(carried, keys, values, valid_keys, queries):
    running, denominator, numerator = carried
    scores = jnp.einsum("qhd,khd->qhk", queries, keys, preferred_element_type=jnp.float32) * SCALE
    scores = jnp.where(valid_keys[None, None, :], scores, -jnp.inf)
    updated = jnp.maximum(running, jnp.max(scores, axis=2))
    rescale = jnp.exp(running - updated)
    weights = jnp.exp(scores - updated[:, :, None])
    denominator = denominator * rescale + jnp.sum(weights, axis=2)
    product = jnp.einsum(
        "qhk,khd->qhd", weights.astype(jnp.bfloat16), values, preferred_element_type=jnp.float32
    )
    numerator = numerator * rescale[:, :, None] + product
    return (updated, denominator, numerator)


def attend_ring(blocks, query_blocks, prompt_ids, image_rows, text_rows):
    group, width = len(blocks), blocks[0].shape[1]
    head_count = width // HEAD_DIM
    key_rows = image_rows + text_rows
    queries = jnp.concatenate([block[:image_rows] for block in blocks[:query_blocks]], axis=0)
    starts = [image_rows if d < query_blocks else 0 for d in range(group)]
    keys, values = (
        jnp.concatenate(
            [block[at + s : at + s + key_rows] for block, s in zip(blocks, starts)], axis=0
        ).reshape(-1, head_count, HEAD_DIM)
        for at in (0, key_rows)
    )
    queries = queries.reshape(-1, head_count, HEAD_DIM)
    seq_count = lax.axis_size("seq")
    group_count = seq_count // group
    own_group = lax.axis_index("seq") // group
    order = (lax.axis_index("seq") % group) ^ jnp.arange(group)
    text_valid = prompt_ids.reshape(seq_count, text_rows) != 0

    def valid_for(source):
        text = lax.dynamic_slice_in_dim(text_valid, source * group, group, 0)[order]
        return jnp.concatenate([jnp.ones((group, image_rows), jnp.bool_), text], axis=1).reshape(-1)

    query_count = queries.shape[0]
    initial = (
        jnp.full((query_count, head_count), -jnp.inf, jnp.float32),
        jnp.zeros((query_count, head_count), jnp.float32),
        jnp.zeros((query_count, head_count, HEAD_DIM), jnp.float32),
    )
    carried = absorb(initial, keys, values, valid_for(own_group), queries)

    def one_turn(turn, state):
        current, keys, values = state
        keys, values = shifted(keys, "seq", group), shifted(values, "seq", group)
        source = (own_group - turn) % group_count
        return (absorb(current, keys, values, valid_for(source), queries), keys, values)

    carried, _, _ = lax.fori_loop(1, group_count, one_turn, (carried, keys, values))
    _, denominator, numerator = carried
    attended = (numerator / denominator[:, :, None]).astype(jnp.bfloat16)
    return attended.reshape(query_blocks, image_rows, width)


def ring_strips(blocks, prompt_ids, image_rows, text_rows):
    group = len(blocks)
    attended = attend_ring(blocks, group, prompt_ids, image_rows, text_rows)
    sides = attended.reshape(2, -1, 2, STRIDE, attended.shape[2])
    return [[sides[p, :, s].reshape(-1, attended.shape[2]) for p in range(2)] for s in range(2)]


def ring_half(blocks, prompt_ids, image_rows, text_rows):
    return list(attend_ring(blocks, len(blocks) // 2, prompt_ids, image_rows, text_rows))


def on_device(query, key_image, value_image, key_text, value_text, prompt_ids, blend, w_out):
    seq_count = lax.axis_size("seq")
    group = math.gcd(HEADS & -HEADS, seq_count)
    heads = HEADS // group - 1
    halfway = group // 2
    image_rows, text_rows = query.shape[1], key_text.shape[1]
    message_rows = 3 * image_rows + 2 * text_rows
    sources = [query[0], key_image[0], key_text[0], value_image[0], value_text[0]]
    sources = [pltpu.with_memory_space_constraint(source, pltpu.HBM) for source in sources]

    blend_there = pltpu.with_memory_space_constraint(blend, pltpu.HBM)
    far, near = tuple(range(halfway, group)), tuple(range(1, halfway))
    received = [None] * group
    for distances in (far, near):
        packed = pack(sources, blend_there, heads, group, distances)
        for distance, message in zip(distances, packed):
            received[distance] = swapped(message, distance)
    weights = load_weights(w_out, [])
    prepared = prepare(sources, blend, prompt_ids, heads, group, [weights])
    received[0], packed, bias = prepared[0], prepared[1:-1], prepared[-1]
    first = received
    second = [packed[0]] + [swapped(hold(packed[d], [first[halfway]]), d) for d in near]
    for distance in far:
        second.append(swapped(hold(packed[distance], first[halfway:] if distance == halfway else first[halfway : halfway + 1]), distance))
    blend_weights = weigh(first, message_rows, image_rows)

    def strips_of(blocks):
        if seq_count == group:
            return attend(blocks, bias, image_rows, text_rows)
        return ring_strips(blocks, prompt_ids[0], image_rows, text_rows)

    def results_of(blocks, after):
        if seq_count == group:
            return attend_half(blocks, bias, image_rows, text_rows, after)
        return ring_half(blocks, prompt_ids[0], image_rows, text_rows)

    def returned(mixed):
        return [mixed[0]] + [swapped(mixed[d], d) for d in range(1, len(mixed))]

    lefts, rights = strips_of(first)
    sides = [
        (left, shifted(right, "win", 1), weight)
        for left, right, weight in zip(lefts, rights, blend_weights[::2])
    ]
    mixed = blend_strips(sides, group)
    begun = returned(mixed)

    results = returned(results_of(second, [mixed[0], weights]))
    left, right = merge(results, group, [])
    from_prev, from_next = shifted(right, "win", 1), shifted(left, "win", -1)
    begins = collect(begun)
    total = project_begin(begins, shifted(begins, "win", -1), weights)
    strips = [left, right, from_prev, from_next]
    return project_end(strips, blend_weights[:2], weights, total)[None]


def solution(mesh):
    tokens = P(("pano", "win"), "seq", None)
    return jax.shard_map(
        on_device,
        mesh=mesh,
        in_specs=(tokens,) * 5 + (P(("pano", "win"), None), P(("pano", "win"), "seq"), P()),
        out_specs=tokens,
        check_vma=False,
    )
```

```python
import functools
import math

import jax
import jax.numpy as jnp
from jax import lax
from jax.experimental import pallas as pl
from jax.experimental.pallas import tpu as pltpu
from jax.sharding import PartitionSpec as P

HEADS = 12
HEAD_DIM = 128
WCOLS = 64
STRIDE = 32
BLEND_TOTAL = 16.0
SCALE = HEAD_DIM ** (-0.5)
EXP2_SCALE = SCALE * math.log2(math.e)
MIB = 1024 * 1024
SMALL = pltpu.CompilerParams(vmem_limit_bytes=16 * MIB)
NO_COST = pl.CostEstimate(flops=0, bytes_accessed=0, transcendentals=0)
LARGE = pltpu.CompilerParams(vmem_limit_bytes=60 * MIB)

ANY = pl.BlockSpec(memory_space=pl.ANY)
VMEM = pl.BlockSpec(memory_space=pltpu.VMEM)


def shifted(block, axis, distance):
    count = lax.axis_size(axis)
    return lax.ppermute(block, axis, [(i, (i + distance) % count) for i in range(count)])


def paired(block, odd):
    count = lax.axis_size("win")
    step = [-1, 1] if odd else [1, -1]
    return lax.ppermute(block, "win", [(i, (i + step[i % 2]) % count) for i in range(count)])


def swapped(block, distance):
    return lax.ppermute(block, "seq", [(i, i ^ distance) for i in range(lax.axis_size("seq"))])


def partner(distance, group):
    position = lax.rem(lax.axis_index("seq"), group)
    result, bit = 0, 1
    while bit < group:
        own = lax.rem(lax.div(position, bit), 2)
        result = result + (1 - own if distance & bit else own) * bit
        bit *= 2
    return result


def start_block(sources, packed, start, sems):
    columns = pl.ds(pl.multiple_of(start * HEAD_DIM, HEAD_DIM), packed.shape[1])
    copies, row = [], 0
    for source in sources:
        rows = source.shape[0]
        copy = pltpu.make_async_copy(
            source.at[:, columns], packed.at[pl.ds(row, rows)], sems.at[len(copies)]
        )
        copy.start()
        copies.append(copy)
        row += rows
    return copies


def store_weights(blend, wide, packed, row):
    wide[...] = jnp.zeros_like(wide)
    wide[:, : blend.shape[1]] = blend[...].astype(jnp.float32)
    rows, width = packed.shape[0] - row, packed.shape[1]
    index = lax.broadcasted_iota(jnp.int32, (rows, 128), 0)
    value = jnp.zeros((rows, 128), jnp.float32)
    for at in range(0, wide.shape[1], 128):
        value = jnp.where(index == at // 128, wide[:, at : at + 128], value)
    packed[row:, :128] = value.astype(packed.dtype)
    if width > 128:
        packed[row:, 128:] = jnp.zeros((rows, width - 128), packed.dtype)


def pack_kernel(heads, group, distances, count, *refs):
    sources, blend = refs[:count], refs[count]
    packed = refs[count + 1 : count + 1 + len(distances)]
    sems, blend_rows, wide = refs[count + 1 + len(distances) :]
    copies = []
    load = pltpu.make_async_copy(blend, blend_rows, sems.at[len(distances), 0])
    load.start()
    for index, distance in enumerate(distances):
        start = partner(distance, group) * heads
        copies += start_block(sources, packed[index], start, sems.at[index])
    load.wait()
    message_rows = sum(source.shape[0] for source in sources)
    for ref in packed:
        store_weights(blend_rows, wide, ref, message_rows)
    for copy in copies:
        copy.wait()


def weight_rows(blend):
    return -(-blend.shape[1] // (16 * 128)) * 16


def wide_shape(blend):
    return (1, -(-blend.shape[1] // 128) * 128)


def pack(sources, blend, heads, group, distances):
    rows = sum(source.shape[0] for source in sources) + weight_rows(blend)
    out = jax.ShapeDtypeStruct((rows, heads * HEAD_DIM), sources[0].dtype)
    return pl.pallas_call(
        functools.partial(pack_kernel, heads, group, distances, len(sources)),
        out_shape=[out] * len(distances),
        in_specs=[ANY] * (len(sources) + 1),
        out_specs=[VMEM] * len(distances),
        scratch_shapes=[
            pltpu.SemaphoreType.DMA((len(distances) + 1, len(sources))),
            pltpu.VMEM(blend.shape, blend.dtype),
            pltpu.VMEM(wide_shape(blend), jnp.float32),
        ],
        compiler_params=SMALL,
        cost_estimate=NO_COST,
        name="pack",
    )(*sources, blend)


def prepare_kernel(heads, group, count, *refs):
    sources, (blend, ids) = refs[:count], refs[count : count + 2]
    packed, (bias, sems, wide) = refs[-4 - group : -3], refs[-3:]
    message_rows = sum(source.shape[0] for source in sources)
    copies = start_block(sources, packed[0], partner(0, group) * heads, sems.at[0])
    for distance in range(group):
        kept = sources if distance < group // 2 else sources[1:]
        start = group * heads + lax.rem(partner(distance, group), group // 2) * 2
        copies += start_block(kept, packed[1 + distance], start, sems.at[1 + distance])
    bias[...] = jnp.where(ids[...] != 0, 0.0, -jnp.inf)
    store_weights(blend, wide, packed[0], message_rows)
    for copy in copies:
        copy.wait()


def prepare(sources, blend, ids, heads, group, after):
    rows = sum(source.shape[0] for source in sources)
    dtype = sources[0].dtype
    outs = [jax.ShapeDtypeStruct((rows + weight_rows(blend), heads * HEAD_DIM), dtype)]
    for distance in range(group):
        kept = rows if distance < group // 2 else rows - sources[0].shape[0]
        outs.append(jax.ShapeDtypeStruct((kept, 2 * HEAD_DIM), dtype))
    outs.append(jax.ShapeDtypeStruct(ids.shape, jnp.float32))
    return pl.pallas_call(
        functools.partial(prepare_kernel, heads, group, len(sources)),
        out_shape=outs,
        in_specs=[ANY] * len(sources) + [VMEM] * 2 + [ANY] * len(after),
        out_specs=[VMEM] * len(outs),
        scratch_shapes=[
            pltpu.SemaphoreType.DMA((len(outs), len(sources))),
            pltpu.VMEM(wide_shape(blend), jnp.float32),
        ],
        compiler_params=SMALL,
        cost_estimate=NO_COST,
        name="prepare",
    )(*sources, blend, ids, *after)


def soften(query, key, value, bias):
    scores = lax.dot_general(
        query, key, (((1,), (1,)), ((), ())), preferred_element_type=jnp.float32
    )
    image_keys = scores.shape[1] - bias.shape[1]
    scores = jnp.concatenate([scores[:, :image_keys], scores[:, image_keys:] + bias], axis=1)
    peak = jnp.max(scores, axis=1, keepdims=True)
    weights = jnp.exp2((scores - peak) * EXP2_SCALE)
    total = jnp.sum(weights, axis=1, keepdims=True)
    result = jnp.dot(weights.astype(jnp.bfloat16), value, preferred_element_type=jnp.float32)
    return (result / total).astype(jnp.bfloat16)


def fill(keys, values, mask, bias, blocks, sources, starts, group, image_rows, text_rows):
    key_rows, texts = image_rows + text_rows, group * text_rows
    for ref, offset in ((keys, 0), (values, key_rows)):
        ref[:texts] = jnp.zeros((texts, ref.shape[1]), ref.dtype)
        for index, (block, source, start) in enumerate(zip(blocks, sources, starts)):
            at, image = start + offset, texts + index * image_rows
            ref[image : image + image_rows] = block[at : at + image_rows]
            text = pl.ds(pl.multiple_of(source * text_rows, text_rows), text_rows)
            ref[text] = block[at + image_rows : at + key_rows]
    lane = lax.broadcasted_iota(jnp.int32, bias.shape, 1)
    here = jnp.zeros(bias.shape, jnp.int32)
    for source in sources:
        inside = (lane >= source * text_rows) & (lane < (source + 1) * text_rows)
        here = jnp.where(inside, 1, here)
    mask[...] = jnp.zeros_like(mask)
    mask[:, :texts] = jnp.where(here == 1, bias[...], -jnp.inf)


def sum_up(query, key, value, mask, peak=None):
    scores = lax.dot_general(
        query, key, (((1,), (1,)), ((), ())), preferred_element_type=jnp.float32
    )
    scores = scores + mask
    highest = jnp.max(scores, axis=1, keepdims=True)
    highest = jnp.broadcast_to(highest, (scores.shape[0], HEAD_DIM))
    if peak is not None:
        highest = jnp.maximum(highest, peak)
    tiles = -(-scores.shape[1] // HEAD_DIM)
    wide = jnp.concatenate([highest] * tiles, axis=1)[:, : scores.shape[1]]
    weights = jnp.exp2((scores - wide) * EXP2_SCALE)
    total = jnp.broadcast_to(jnp.sum(weights, axis=1, keepdims=True), highest.shape)
    product = jnp.dot(weights.astype(jnp.bfloat16), value, preferred_element_type=jnp.float32)
    return product, total, highest


def early_kernel(group, image_rows, text_rows, bias, *refs):
    halfway = group // 2
    blocks = refs[: group - 1]
    products, totals, peaks, keys, values, mask = refs[-6:]
    distances = [d for d in range(group) if d != halfway]
    sources = [partner(d, group) for d in distances]
    starts = [image_rows if d < halfway else 0 for d in distances]
    fill(keys, values, mask, bias, blocks, sources, starts, group, image_rows, text_rows)
    for at in range(0, keys.shape[1], HEAD_DIM):
        head = slice(at, at + HEAD_DIM)
        for index in range(halfway):
            rows = slice(index * image_rows, (index + 1) * image_rows)
            product, total, peak = sum_up(
                blocks[index][:image_rows, head],
                keys[:, head],
                values[:, head],
                mask[...],
            )
            products[rows, head] = product
            totals[rows, head] = total
            peaks[rows, head] = peak


def late_kernel(group, image_rows, text_rows, index, bias, products, totals, peaks, *refs):
    halfway = group // 2
    near, block, out, keys, values, mask = refs
    sources = [partner(halfway, group)]
    fill(keys, values, mask, bias, [block], sources, [0], group, image_rows, text_rows)
    for at in range(0, keys.shape[1], HEAD_DIM):
        head = slice(at, at + HEAD_DIM)
        rows = slice(index * image_rows, (index + 1) * image_rows)
        before = peaks[rows, head]
        product, total, peak = sum_up(
            near[:image_rows, head],
            keys[:, head],
            values[:, head],
            mask[...],
            before,
        )
        scale = jnp.exp2((before - peak) * EXP2_SCALE)
        total += totals[rows, head] * scale
        product += products[rows, head] * scale
        out[:, head] = (product / total).astype(jnp.bfloat16)


def attend_half(blocks, bias, image_rows, text_rows, after):
    group, width = len(blocks), blocks[0].shape[1]
    halfway = group // 2
    near, last = list(blocks[:halfway]), blocks[halfway]
    others = near + list(blocks[halfway + 1 :])
    texts = group * text_rows
    total = jax.ShapeDtypeStruct((halfway * image_rows, width), jnp.float32)
    count = len(others) * image_rows + texts
    keys, mask = pltpu.VMEM((count, width), jnp.bfloat16), pltpu.VMEM((1, count), jnp.float32)
    sums = pl.pallas_call(
        functools.partial(early_kernel, group, image_rows, text_rows),
        out_shape=[total] * 3,
        in_specs=[VMEM] * group + [ANY] * len(after),
        out_specs=[VMEM] * 3,
        scratch_shapes=[keys, keys, mask],
        compiler_params=SMALL,
        cost_estimate=NO_COST,
        name="attend_early",
    )(bias, *others, *after)
    count = image_rows + texts
    keys, mask = pltpu.VMEM((count, width), jnp.bfloat16), pltpu.VMEM((1, count), jnp.float32)
    results = [None] * halfway
    for index in reversed(range(halfway)):
        results[index] = pl.pallas_call(
            functools.partial(late_kernel, group, image_rows, text_rows, index),
            out_shape=jax.ShapeDtypeStruct((image_rows, width), jnp.bfloat16),
            in_specs=[VMEM] * 6,
            out_specs=VMEM,
            scratch_shapes=[keys, keys, mask],
            compiler_params=SMALL,
            cost_estimate=NO_COST,
            name="attend_late",
        )(bias, *sums, near[index], last)
    return results


def merge_kernel(group, *refs):
    blocks, (left, right, first, second) = refs[: group // 2], refs[-4:]
    width = blocks[0].shape[1]
    even = lax.rem(lax.axis_index("win"), 2) == 0
    for distance, block in enumerate(blocks):
        start = lax.rem(partner(distance, group), group // 2) * width
        columns = pl.ds(pl.multiple_of(start, HEAD_DIM), width)
        for row in range(block.shape[0] // WCOLS):
            for side, out in enumerate((left, right)):
                at = row * WCOLS + side * STRIDE
                out[pl.ds(row * STRIDE, STRIDE), columns] = block[at : at + STRIDE]

    @pl.when(even)
    def _():
        first[...], second[...] = right[...], left[...]

    @pl.when(jnp.logical_not(even))
    def _():
        first[...], second[...] = left[...], right[...]


def merge(blocks, group):
    rows, width = blocks[0].shape
    strip = jax.ShapeDtypeStruct((rows // 2, len(blocks) * width), jnp.bfloat16)
    return pl.pallas_call(
        functools.partial(merge_kernel, group),
        out_shape=[strip] * 4,
        in_specs=[VMEM] * len(blocks),
        out_specs=[VMEM] * 4,
        compiler_params=SMALL,
        cost_estimate=NO_COST,
        name="merge",
    )(*blocks)


def attend_kernel(group, image_rows, text_rows, bias, *refs):
    blocks, lefts, rights, (keys, values) = refs[:group], refs[-6:-4], refs[-4:-2], refs[-2:]
    key_rows = image_rows + text_rows
    for distance, block in enumerate(blocks):
        source = partner(distance, group)
        image = pl.ds(distance * image_rows, image_rows)
        text = pl.ds(pl.multiple_of(group * image_rows + source * text_rows, text_rows), text_rows)
        for ref, at in ((keys, image_rows), (values, image_rows + key_rows)):
            ref[image] = block[at : at + image_rows]
            ref[text] = block[at + image_rows : at + key_rows]
    half = image_rows // 2
    for at_head in range(0, keys.shape[1], HEAD_DIM):
        head = slice(at_head, at_head + HEAD_DIM)
        for distance, block in enumerate(blocks):
            result = soften(block[:image_rows, head], keys[:, head], values[:, head], bias[...])
            piece, place = divmod(distance, group // 2)
            left, right = lefts[piece], rights[piece]
            for row in range(image_rows // WCOLS):
                at = place * half + row * STRIDE
                left[at : at + STRIDE, head] = result[row * WCOLS : row * WCOLS + STRIDE]
                right[at : at + STRIDE, head] = result[row * WCOLS + STRIDE : (row + 1) * WCOLS]


def attend(blocks, bias, image_rows, text_rows):
    group, width = len(blocks), blocks[0].shape[1]
    strip = jax.ShapeDtypeStruct((group // 2 * image_rows // 2, width), jnp.bfloat16)
    keys = pltpu.VMEM((group * (image_rows + text_rows), width), jnp.bfloat16)
    strips = pl.pallas_call(
        functools.partial(attend_kernel, group, image_rows, text_rows),
        out_shape=[strip] * 4,
        in_specs=[VMEM] * (1 + group),
        out_specs=[VMEM] * 4,
        scratch_shapes=[keys, keys],
        compiler_params=SMALL,
        cost_estimate=NO_COST,
        name="attend",
    )(bias, *blocks)
    return strips[:2], strips[2:]


def weigh_kernel(group, weight_row, image_rows, *refs):
    blocks, outs = refs[:group], refs[group:]
    half = image_rows // 2
    for distance in range(group):
        columns = blocks[distance][weight_row : weight_row + 16, :128].astype(jnp.float32).T
        for row in range(image_rows // WCOLS):
            column, start = row * WCOLS // 128, row * WCOLS % 128
            piece, place = divmod(distance, group // 2)
            at = place * half + row * STRIDE
            for side, out in enumerate(outs[2 * piece : 2 * piece + 2]):
                first = start + side * STRIDE
                out[at : at + STRIDE] = jnp.broadcast_to(
                    columns[first : first + STRIDE, column : column + 1], (STRIDE, HEAD_DIM)
                )


def weigh(blocks, weight_row, image_rows):
    group = len(blocks)
    out = jax.ShapeDtypeStruct((group // 2 * image_rows // 2, HEAD_DIM), jnp.float32)
    return pl.pallas_call(
        functools.partial(weigh_kernel, group, weight_row, image_rows),
        out_shape=[out] * 4,
        in_specs=[VMEM] * group,
        out_specs=[VMEM] * 4,
        compiler_params=SMALL,
        cost_estimate=NO_COST,
        name="weigh",
    )(*blocks)


def blend_kernel(count, *refs):
    sides, outs = refs[: 3 * count], refs[3 * count :]
    half, blocks = outs[0].shape[0], len(outs) // count
    for index, out in enumerate(outs):
        own, other, weight_ref = sides[index // blocks * 3 : index // blocks * 3 + 3]
        rows = pl.ds(index % blocks * half, half)
        for at_head in range(0, own.shape[1], HEAD_DIM):
            head = pl.ds(at_head, HEAD_DIM)
            weight = weight_ref[rows]
            mixed = weight * own[rows, head].astype(jnp.float32)
            mixed += (BLEND_TOTAL - weight) * other[rows, head].astype(jnp.float32)
            out[:, head] = (mixed * (1.0 / BLEND_TOTAL)).astype(jnp.bfloat16)


def blend_strips(sides, blocks):
    rows, width = sides[0][0].shape
    out = jax.ShapeDtypeStruct((len(sides) * rows // blocks, width), jnp.bfloat16)
    return pl.pallas_call(
        functools.partial(blend_kernel, len(sides)),
        out_shape=[out] * blocks,
        in_specs=[VMEM] * (3 * len(sides)),
        out_specs=[VMEM] * blocks,
        compiler_params=SMALL,
        cost_estimate=NO_COST,
        name="blend",
    )(*sum(sides, ()))


def load_kernel(w_out, *refs):
    out, sem = refs[-2:]
    copy = pltpu.make_async_copy(w_out, out, sem)
    copy.start()
    copy.wait()


def load_weights(w_out, after):
    return pl.pallas_call(
        load_kernel,
        out_shape=jax.ShapeDtypeStruct(w_out.shape, w_out.dtype),
        in_specs=[ANY] * (1 + len(after)),
        out_specs=VMEM,
        scratch_shapes=[pltpu.SemaphoreType.DMA],
        compiler_params=SMALL,
        cost_estimate=NO_COST,
        name="load_weights",
    )(w_out, *after)


def hold_kernel(source, *refs):
    refs[-1][...] = source[...]


def hold(array, after):
    return pl.pallas_call(
        hold_kernel,
        out_shape=jax.ShapeDtypeStruct(array.shape, array.dtype),
        in_specs=[VMEM] + [ANY] * len(after),
        out_specs=VMEM,
        compiler_params=SMALL,
        cost_estimate=NO_COST,
        name="hold",
    )(array, *after)


def collect_kernel(group, *refs):
    blocks, out = refs[:group], refs[-1]
    width = blocks[0].shape[1]
    for distance in range(group):
        start = pl.multiple_of(partner(distance, group) * width, HEAD_DIM)
        out[:, pl.ds(start, width)] = blocks[distance][...]


def collect(blocks):
    group = len(blocks)
    rows, width = blocks[0].shape
    return pl.pallas_call(
        functools.partial(collect_kernel, group),
        out_shape=jax.ShapeDtypeStruct((rows, group * width), blocks[0].dtype),
        in_specs=[VMEM] * group,
        out_specs=VMEM,
        compiler_params=SMALL,
        cost_estimate=NO_COST,
        name="collect",
    )(*blocks)


TILES = 6


def begin_kernel(left, right, weights, total, features):
    depth = features.shape[1]
    for row in range(features.shape[0] // WCOLS):
        strip = slice(row * STRIDE, (row + 1) * STRIDE)
        at = row * WCOLS
        features[at : at + STRIDE] = left[strip]
        features[at + STRIDE : at + WCOLS] = right[strip]
    tile = total.shape[1] // TILES
    for at in range(0, total.shape[1], tile):
        total[:, at : at + tile] = jnp.dot(
            features[...], weights[:depth, at : at + tile], preferred_element_type=jnp.float32
        )


def project_begin(left, right, weights):
    rows, depth = left.shape
    return pl.pallas_call(
        begin_kernel,
        out_shape=jax.ShapeDtypeStruct((2 * rows, weights.shape[1]), jnp.float32),
        in_specs=[VMEM] * 3,
        out_specs=VMEM,
        scratch_shapes=[pltpu.VMEM((2 * rows, depth), jnp.bfloat16)],
        compiler_params=SMALL,
        cost_estimate=NO_COST,
        name="project_begin",
    )(left, right, weights)


def end_kernel(left, right, first_in, second_in, *refs):
    weight_left, weight_right, weights, total, out, features, result, sems = refs
    rows = left.shape[0]
    even = lax.rem(lax.axis_index("win"), 2) == 0
    for side, (own, other, weight_ref) in enumerate(
        ((left, (second_in, first_in), weight_left), (right, (first_in, second_in), weight_right))
    ):
        weight = weight_ref[:rows]
        for at in range(0, own.shape[1], HEAD_DIM):
            head = pl.ds(at, HEAD_DIM)
            mixed = weight * own[:, head].astype(jnp.float32)
            theirs = [ref[:, head].astype(jnp.float32) for ref in other]
            mixed += (BLEND_TOTAL - weight) * jnp.where(even, *theirs)
            mixed = (mixed * (1.0 / BLEND_TOTAL)).astype(jnp.bfloat16)
            for row in range(rows // STRIDE):
                start = row * WCOLS + side * STRIDE
                features[pl.ds(start, STRIDE), head] = mixed[row * STRIDE : (row + 1) * STRIDE]
    tile = result.shape[1] // TILES
    first = weights.shape[0] - features.shape[1]
    copies = []
    for at in range(0, result.shape[1], tile):
        columns = pl.ds(at, tile)
        product = jnp.dot(
            features[...], weights[first:, at : at + tile], preferred_element_type=jnp.float32
        )
        result[:, columns] = (total[:, columns] + product).astype(jnp.bfloat16)
        copy = pltpu.make_async_copy(
            result.at[:, columns], out.at[:, columns], sems.at[len(copies)]
        )
        copy.start()
        copies.append(copy)
    for copy in copies:
        copy.wait()


def project_end(strips, blend_weights, weights, total):
    rows, width = total.shape
    return pl.pallas_call(
        end_kernel,
        out_shape=jax.ShapeDtypeStruct((rows, width), jnp.bfloat16),
        in_specs=[VMEM] * 8,
        out_specs=ANY,
        scratch_shapes=[
            pltpu.VMEM((rows, strips[0].shape[1]), jnp.bfloat16),
            pltpu.VMEM((rows, width), jnp.bfloat16),
            pltpu.SemaphoreType.DMA((TILES,)),
        ],
        compiler_params=SMALL,
        cost_estimate=NO_COST,
        name="project_end",
    )(*strips, *blend_weights, weights, total)


def absorb(carried, keys, values, valid_keys, queries):
    running, denominator, numerator = carried
    scores = jnp.einsum("qhd,khd->qhk", queries, keys, preferred_element_type=jnp.float32) * SCALE
    scores = jnp.where(valid_keys[None, None, :], scores, -jnp.inf)
    updated = jnp.maximum(running, jnp.max(scores, axis=2))
    rescale = jnp.exp(running - updated)
    weights = jnp.exp(scores - updated[:, :, None])
    denominator = denominator * rescale + jnp.sum(weights, axis=2)
    product = jnp.einsum(
        "qhk,khd->qhd", weights.astype(jnp.bfloat16), values, preferred_element_type=jnp.float32
    )
    numerator = numerator * rescale[:, :, None] + product
    return (updated, denominator, numerator)


def attend_ring(blocks, query_blocks, prompt_ids, image_rows, text_rows):
    group, width = len(blocks), blocks[0].shape[1]
    head_count = width // HEAD_DIM
    key_rows = image_rows + text_rows
    queries = jnp.concatenate([block[:image_rows] for block in blocks[:query_blocks]], axis=0)
    starts = [image_rows if d < query_blocks else 0 for d in range(group)]
    keys, values = (
        jnp.concatenate(
            [block[at + s : at + s + key_rows] for block, s in zip(blocks, starts)], axis=0
        ).reshape(-1, head_count, HEAD_DIM)
        for at in (0, key_rows)
    )
    queries = queries.reshape(-1, head_count, HEAD_DIM)
    seq_count = lax.axis_size("seq")
    group_count = seq_count // group
    own_group = lax.axis_index("seq") // group
    order = (lax.axis_index("seq") % group) ^ jnp.arange(group)
    text_valid = prompt_ids.reshape(seq_count, text_rows) != 0

    def valid_for(source):
        text = lax.dynamic_slice_in_dim(text_valid, source * group, group, 0)[order]
        return jnp.concatenate([jnp.ones((group, image_rows), jnp.bool_), text], axis=1).reshape(-1)

    query_count = queries.shape[0]
    initial = (
        jnp.full((query_count, head_count), -jnp.inf, jnp.float32),
        jnp.zeros((query_count, head_count), jnp.float32),
        jnp.zeros((query_count, head_count, HEAD_DIM), jnp.float32),
    )
    carried = absorb(initial, keys, values, valid_for(own_group), queries)

    def one_turn(turn, state):
        current, keys, values = state
        keys, values = shifted(keys, "seq", group), shifted(values, "seq", group)
        source = (own_group - turn) % group_count
        return (absorb(current, keys, values, valid_for(source), queries), keys, values)

    carried, _, _ = lax.fori_loop(1, group_count, one_turn, (carried, keys, values))
    _, denominator, numerator = carried
    attended = (numerator / denominator[:, :, None]).astype(jnp.bfloat16)
    return attended.reshape(query_blocks, image_rows, width)


def ring_strips(blocks, prompt_ids, image_rows, text_rows):
    group = len(blocks)
    attended = attend_ring(blocks, group, prompt_ids, image_rows, text_rows)
    sides = attended.reshape(2, -1, 2, STRIDE, attended.shape[2])
    return [[sides[p, :, s].reshape(-1, attended.shape[2]) for p in range(2)] for s in range(2)]


def ring_half(blocks, prompt_ids, image_rows, text_rows):
    return list(attend_ring(blocks, len(blocks) // 2, prompt_ids, image_rows, text_rows))


def on_device(query, key_image, value_image, key_text, value_text, prompt_ids, blend, w_out):
    seq_count = lax.axis_size("seq")
    group = math.gcd(HEADS & -HEADS, seq_count)
    heads = HEADS // group - 1
    halfway = group // 2
    image_rows, text_rows = query.shape[1], key_text.shape[1]
    message_rows = 3 * image_rows + 2 * text_rows
    sources = [query[0], key_image[0], key_text[0], value_image[0], value_text[0]]
    sources = [pltpu.with_memory_space_constraint(source, pltpu.HBM) for source in sources]

    blend_there = pltpu.with_memory_space_constraint(blend, pltpu.HBM)
    far, near = tuple(range(halfway, group)), tuple(range(1, halfway))
    received = [None] * group
    for distances in (far, near):
        packed = pack(sources, blend_there, heads, group, distances)
        for distance, message in zip(distances, packed):
            received[distance] = swapped(message, distance)
    weights = load_weights(w_out, [])
    prepared = prepare(sources, blend, prompt_ids, heads, group, [weights])
    received[0], packed, bias = prepared[0], prepared[1:-1], prepared[-1]
    first = received
    second = [packed[0]] + [swapped(hold(packed[d], [first[halfway]]), d) for d in near]
    for distance in far:
        second.append(swapped(hold(packed[distance], first[halfway:] if distance == halfway else first[halfway : halfway + 1]), distance))
    blend_weights = weigh(first, message_rows, image_rows)

    def strips_of(blocks):
        if seq_count == group:
            return attend(blocks, bias, image_rows, text_rows)
        return ring_strips(blocks, prompt_ids[0], image_rows, text_rows)

    def results_of(blocks, after):
        if seq_count == group:
            return attend_half(blocks, bias, image_rows, text_rows, after)
        return ring_half(blocks, prompt_ids[0], image_rows, text_rows)

    def returned(mixed):
        return [mixed[0]] + [swapped(mixed[d], d) for d in range(1, len(mixed))]

    lefts, rights = strips_of(first)
    sides = [
        (left, shifted(right, "win", 1), weight)
        for left, right, weight in zip(lefts, rights, blend_weights[::2])
    ]
    mixed = blend_strips(sides, group)
    begun = returned(mixed)

    results = returned(results_of(second, [mixed[0], weights]))
    left, right, to_first, to_second = merge(results, group)
    second_in, first_in = paired(to_second, True), paired(to_first, False)
    begins = collect(begun)
    total = project_begin(begins, shifted(begins, "win", -1), weights)
    strips = [left, right, first_in, second_in]
    return project_end(strips, blend_weights[:2], weights, total)[None]


def solution(mesh):
    tokens = P(("pano", "win"), "seq", None)
    return jax.shard_map(
        on_device,
        mesh=mesh,
        in_specs=(tokens,) * 5 + (P(("pano", "win"), None), P(("pano", "win"), "seq"), P()),
        out_specs=tokens,
        check_vma=False,
    )
```

```python
import functools
import math

import jax
import jax.numpy as jnp
from jax import lax
from jax.experimental import pallas as pl
from jax.experimental.pallas import tpu as pltpu
from jax.sharding import PartitionSpec as P

HEADS = 12
HEAD_DIM = 128
WCOLS = 64
STRIDE = 32
BLEND_TOTAL = 16.0
SCALE = HEAD_DIM ** (-0.5)
EXP2_SCALE = SCALE * math.log2(math.e)
MIB = 1024 * 1024
SMALL = pltpu.CompilerParams(vmem_limit_bytes=16 * MIB)
NO_COST = pl.CostEstimate(flops=0, bytes_accessed=0, transcendentals=0)
LARGE = pltpu.CompilerParams(vmem_limit_bytes=60 * MIB)

ANY = pl.BlockSpec(memory_space=pl.ANY)
VMEM = pl.BlockSpec(memory_space=pltpu.VMEM)


def shifted(block, axis, distance):
    count = lax.axis_size(axis)
    return lax.ppermute(block, axis, [(i, (i + distance) % count) for i in range(count)])


def paired(block, odd):
    count = lax.axis_size("win")
    step = [-1, 1] if odd else [1, -1]
    return lax.ppermute(block, "win", [(i, (i + step[i % 2]) % count) for i in range(count)])


def swapped(block, distance):
    return lax.ppermute(block, "seq", [(i, i ^ distance) for i in range(lax.axis_size("seq"))])


def partner(distance, group):
    position = lax.rem(lax.axis_index("seq"), group)
    result, bit = 0, 1
    while bit < group:
        own = lax.rem(lax.div(position, bit), 2)
        result = result + (1 - own if distance & bit else own) * bit
        bit *= 2
    return result


def start_block(sources, packed, start, sems):
    columns = pl.ds(pl.multiple_of(start * HEAD_DIM, HEAD_DIM), packed.shape[1])
    copies, row = [], 0
    for source in sources:
        rows = source.shape[0]
        copy = pltpu.make_async_copy(
            source.at[:, columns], packed.at[pl.ds(row, rows)], sems.at[len(copies)]
        )
        copy.start()
        copies.append(copy)
        row += rows
    return copies


def store_weights(blend, wide, packed, row):
    wide[...] = jnp.zeros_like(wide)
    wide[:, : blend.shape[1]] = blend[...].astype(jnp.float32)
    rows, width = packed.shape[0] - row, packed.shape[1]
    index = lax.broadcasted_iota(jnp.int32, (rows, 128), 0)
    value = jnp.zeros((rows, 128), jnp.float32)
    for at in range(0, wide.shape[1], 128):
        value = jnp.where(index == at // 128, wide[:, at : at + 128], value)
    packed[row:, :128] = value.astype(packed.dtype)
    if width > 128:
        packed[row:, 128:] = jnp.zeros((rows, width - 128), packed.dtype)


def pack_kernel(heads, group, distances, count, *refs):
    sources, blend = refs[:count], refs[count]
    packed = refs[count + 1 : count + 1 + len(distances)]
    sems, blend_rows, wide = refs[count + 1 + len(distances) :]
    copies = []
    load = pltpu.make_async_copy(blend, blend_rows, sems.at[len(distances), 0])
    load.start()
    for index, distance in enumerate(distances):
        start = partner(distance, group) * heads
        copies += start_block(sources, packed[index], start, sems.at[index])
    load.wait()
    message_rows = sum(source.shape[0] for source in sources)
    for ref in packed:
        store_weights(blend_rows, wide, ref, message_rows)
    for copy in copies:
        copy.wait()


def weight_rows(blend):
    return -(-blend.shape[1] // (16 * 128)) * 16


def wide_shape(blend):
    return (1, -(-blend.shape[1] // 128) * 128)


def pack(sources, blend, heads, group, distances):
    rows = sum(source.shape[0] for source in sources) + weight_rows(blend)
    out = jax.ShapeDtypeStruct((rows, heads * HEAD_DIM), sources[0].dtype)
    return pl.pallas_call(
        functools.partial(pack_kernel, heads, group, distances, len(sources)),
        out_shape=[out] * len(distances),
        in_specs=[ANY] * (len(sources) + 1),
        out_specs=[VMEM] * len(distances),
        scratch_shapes=[
            pltpu.SemaphoreType.DMA((len(distances) + 1, len(sources))),
            pltpu.VMEM(blend.shape, blend.dtype),
            pltpu.VMEM(wide_shape(blend), jnp.float32),
        ],
        compiler_params=SMALL,
        cost_estimate=NO_COST,
        name="pack",
    )(*sources, blend)


def prepare_kernel(heads, group, count, *refs):
    sources, (blend, ids) = refs[:count], refs[count : count + 2]
    packed, (bias, sems, wide) = refs[-4 - group : -3], refs[-3:]
    message_rows = sum(source.shape[0] for source in sources)
    copies = start_block(sources, packed[0], partner(0, group) * heads, sems.at[0])
    for distance in range(group):
        kept = sources if distance < group // 2 else sources[1:]
        start = group * heads + lax.rem(partner(distance, group), group // 2) * 2
        copies += start_block(kept, packed[1 + distance], start, sems.at[1 + distance])
    bias[...] = jnp.where(ids[...] != 0, 0.0, -jnp.inf)
    store_weights(blend, wide, packed[0], message_rows)
    for copy in copies:
        copy.wait()


def prepare(sources, blend, ids, heads, group, after):
    rows = sum(source.shape[0] for source in sources)
    dtype = sources[0].dtype
    outs = [jax.ShapeDtypeStruct((rows + weight_rows(blend), heads * HEAD_DIM), dtype)]
    for distance in range(group):
        kept = rows if distance < group // 2 else rows - sources[0].shape[0]
        outs.append(jax.ShapeDtypeStruct((kept, 2 * HEAD_DIM), dtype))
    outs.append(jax.ShapeDtypeStruct(ids.shape, jnp.float32))
    return pl.pallas_call(
        functools.partial(prepare_kernel, heads, group, len(sources)),
        out_shape=outs,
        in_specs=[ANY] * len(sources) + [VMEM] * 2 + [ANY] * len(after),
        out_specs=[VMEM] * len(outs),
        scratch_shapes=[
            pltpu.SemaphoreType.DMA((len(outs), len(sources))),
            pltpu.VMEM(wide_shape(blend), jnp.float32),
        ],
        compiler_params=SMALL,
        cost_estimate=NO_COST,
        name="prepare",
    )(*sources, blend, ids, *after)


def soften(query, key, value, bias):
    scores = lax.dot_general(
        query, key, (((1,), (1,)), ((), ())), preferred_element_type=jnp.float32
    )
    image_keys = scores.shape[1] - bias.shape[1]
    scores = jnp.concatenate([scores[:, :image_keys], scores[:, image_keys:] + bias], axis=1)
    peak = jnp.max(scores, axis=1, keepdims=True)
    weights = jnp.exp2((scores - peak) * EXP2_SCALE)
    total = jnp.sum(weights, axis=1, keepdims=True)
    result = jnp.dot(weights.astype(jnp.bfloat16), value, preferred_element_type=jnp.float32)
    return (result / total).astype(jnp.bfloat16)


def fill(keys, values, mask, bias, blocks, sources, starts, group, image_rows, text_rows):
    key_rows, texts = image_rows + text_rows, group * text_rows
    for ref, offset in ((keys, 0), (values, key_rows)):
        ref[:texts] = jnp.zeros((texts, ref.shape[1]), ref.dtype)
        for index, (block, source, start) in enumerate(zip(blocks, sources, starts)):
            at, image = start + offset, texts + index * image_rows
            ref[image : image + image_rows] = block[at : at + image_rows]
            text = pl.ds(pl.multiple_of(source * text_rows, text_rows), text_rows)
            ref[text] = block[at + image_rows : at + key_rows]
    lane = lax.broadcasted_iota(jnp.int32, bias.shape, 1)
    here = jnp.zeros(bias.shape, jnp.int32)
    for source in sources:
        inside = (lane >= source * text_rows) & (lane < (source + 1) * text_rows)
        here = jnp.where(inside, 1, here)
    mask[...] = jnp.zeros_like(mask)
    mask[:, :texts] = jnp.where(here == 1, bias[...], -jnp.inf)


def sum_up(query, key, value, mask, peak=None):
    scores = lax.dot_general(
        query, key, (((1,), (1,)), ((), ())), preferred_element_type=jnp.float32
    )
    scores = scores + mask
    highest = jnp.max(scores, axis=1, keepdims=True)
    highest = jnp.broadcast_to(highest, (scores.shape[0], HEAD_DIM))
    if peak is not None:
        highest = jnp.maximum(highest, peak)
    tiles = -(-scores.shape[1] // HEAD_DIM)
    wide = jnp.concatenate([highest] * tiles, axis=1)[:, : scores.shape[1]]
    weights = jnp.exp2((scores - wide) * EXP2_SCALE)
    total = jnp.broadcast_to(jnp.sum(weights, axis=1, keepdims=True), highest.shape)
    product = jnp.dot(weights.astype(jnp.bfloat16), value, preferred_element_type=jnp.float32)
    return product, total, highest


def early_kernel(group, image_rows, text_rows, bias, *refs):
    halfway = group // 2
    blocks = refs[: group - 1]
    products, totals, peaks, keys, values, mask = refs[-6:]
    distances = [d for d in range(group) if d != halfway]
    sources = [partner(d, group) for d in distances]
    starts = [image_rows if d < halfway else 0 for d in distances]
    fill(keys, values, mask, bias, blocks, sources, starts, group, image_rows, text_rows)
    for at in range(0, keys.shape[1], HEAD_DIM):
        head = slice(at, at + HEAD_DIM)
        for index in range(halfway):
            rows = slice(index * image_rows, (index + 1) * image_rows)
            product, total, peak = sum_up(
                blocks[index][:image_rows, head],
                keys[:, head],
                values[:, head],
                mask[...],
            )
            products[rows, head] = product
            totals[rows, head] = total
            peaks[rows, head] = peak


def late_kernel(group, image_rows, text_rows, index, bias, products, totals, peaks, *refs):
    halfway = group // 2
    near, block, out, keys, values, mask = refs
    sources = [partner(halfway, group)]
    fill(keys, values, mask, bias, [block], sources, [0], group, image_rows, text_rows)
    for at in range(0, keys.shape[1], HEAD_DIM):
        head = slice(at, at + HEAD_DIM)
        rows = slice(index * image_rows, (index + 1) * image_rows)
        before = peaks[rows, head]
        product, total, peak = sum_up(
            near[:image_rows, head],
            keys[:, head],
            values[:, head],
            mask[...],
            before,
        )
        scale = jnp.exp2((before - peak) * EXP2_SCALE)
        total += totals[rows, head] * scale
        product += products[rows, head] * scale
        out[:, head] = (product / total).astype(jnp.bfloat16)


def attend_half(blocks, bias, image_rows, text_rows, after):
    group, width = len(blocks), blocks[0].shape[1]
    halfway = group // 2
    near, last = list(blocks[:halfway]), blocks[halfway]
    others = near + list(blocks[halfway + 1 :])
    texts = group * text_rows
    total = jax.ShapeDtypeStruct((halfway * image_rows, width), jnp.float32)
    count = len(others) * image_rows + texts
    keys, mask = pltpu.VMEM((count, width), jnp.bfloat16), pltpu.VMEM((1, count), jnp.float32)
    sums = pl.pallas_call(
        functools.partial(early_kernel, group, image_rows, text_rows),
        out_shape=[total] * 3,
        in_specs=[VMEM] * group + [ANY] * len(after),
        out_specs=[VMEM] * 3,
        scratch_shapes=[keys, keys, mask],
        compiler_params=SMALL,
        cost_estimate=NO_COST,
        name="attend_early",
    )(bias, *others, *after)
    count = image_rows + texts
    keys, mask = pltpu.VMEM((count, width), jnp.bfloat16), pltpu.VMEM((1, count), jnp.float32)
    results = [None] * halfway
    for index in reversed(range(halfway)):
        results[index] = pl.pallas_call(
            functools.partial(late_kernel, group, image_rows, text_rows, index),
            out_shape=jax.ShapeDtypeStruct((image_rows, width), jnp.bfloat16),
            in_specs=[VMEM] * 6,
            out_specs=VMEM,
            scratch_shapes=[keys, keys, mask],
            compiler_params=SMALL,
            cost_estimate=NO_COST,
            name="attend_late",
        )(bias, *sums, near[index], last)
    return results


def merge_kernel(group, *refs):
    blocks, (left, right, first, second) = refs[: group // 2], refs[-4:]
    width = blocks[0].shape[1]
    even = lax.rem(lax.axis_index("win"), 2) == 0
    for distance, block in enumerate(blocks):
        start = lax.rem(partner(distance, group), group // 2) * width
        columns = pl.ds(pl.multiple_of(start, HEAD_DIM), width)
        for row in range(block.shape[0] // WCOLS):
            for side, out in enumerate((left, right)):
                at = row * WCOLS + side * STRIDE
                out[pl.ds(row * STRIDE, STRIDE), columns] = block[at : at + STRIDE]

    @pl.when(even)
    def _():
        first[...], second[...] = right[...], left[...]

    @pl.when(jnp.logical_not(even))
    def _():
        first[...], second[...] = left[...], right[...]


def merge(blocks, group):
    rows, width = blocks[0].shape
    strip = jax.ShapeDtypeStruct((rows // 2, len(blocks) * width), jnp.bfloat16)
    return pl.pallas_call(
        functools.partial(merge_kernel, group),
        out_shape=[strip] * 4,
        in_specs=[VMEM] * len(blocks),
        out_specs=[VMEM] * 4,
        compiler_params=SMALL,
        cost_estimate=NO_COST,
        name="merge",
    )(*blocks)


def attend_kernel(group, image_rows, text_rows, bias, *refs):
    blocks, lefts, rights, (keys, values) = refs[:group], refs[-6:-4], refs[-4:-2], refs[-2:]
    key_rows = image_rows + text_rows
    for distance, block in enumerate(blocks):
        source = partner(distance, group)
        image = pl.ds(distance * image_rows, image_rows)
        text = pl.ds(pl.multiple_of(group * image_rows + source * text_rows, text_rows), text_rows)
        for ref, at in ((keys, image_rows), (values, image_rows + key_rows)):
            ref[image] = block[at : at + image_rows]
            ref[text] = block[at + image_rows : at + key_rows]
    half = image_rows // 2
    for at_head in range(0, keys.shape[1], HEAD_DIM):
        head = slice(at_head, at_head + HEAD_DIM)
        for distance, block in enumerate(blocks):
            result = soften(block[:image_rows, head], keys[:, head], values[:, head], bias[...])
            piece, place = divmod(distance, group // 2)
            left, right = lefts[piece], rights[piece]
            for row in range(image_rows // WCOLS):
                at = place * half + row * STRIDE
                left[at : at + STRIDE, head] = result[row * WCOLS : row * WCOLS + STRIDE]
                right[at : at + STRIDE, head] = result[row * WCOLS + STRIDE : (row + 1) * WCOLS]


def attend(blocks, bias, image_rows, text_rows):
    group, width = len(blocks), blocks[0].shape[1]
    strip = jax.ShapeDtypeStruct((group // 2 * image_rows // 2, width), jnp.bfloat16)
    keys = pltpu.VMEM((group * (image_rows + text_rows), width), jnp.bfloat16)
    strips = pl.pallas_call(
        functools.partial(attend_kernel, group, image_rows, text_rows),
        out_shape=[strip] * 4,
        in_specs=[VMEM] * (1 + group),
        out_specs=[VMEM] * 4,
        scratch_shapes=[keys, keys],
        compiler_params=SMALL,
        cost_estimate=NO_COST,
        name="attend",
    )(bias, *blocks)
    return strips[:2], strips[2:]


def weigh_kernel(group, weight_row, image_rows, *refs):
    blocks, outs = refs[:group], refs[group:]
    half = image_rows // 2
    for distance in range(group):
        columns = blocks[distance][weight_row : weight_row + 16, :128].astype(jnp.float32).T
        for row in range(image_rows // WCOLS):
            column, start = row * WCOLS // 128, row * WCOLS % 128
            piece, place = divmod(distance, group // 2)
            at = place * half + row * STRIDE
            for side, out in enumerate(outs[2 * piece : 2 * piece + 2]):
                first = start + side * STRIDE
                out[at : at + STRIDE] = jnp.broadcast_to(
                    columns[first : first + STRIDE, column : column + 1], (STRIDE, HEAD_DIM)
                )


def weigh(blocks, weight_row, image_rows):
    group = len(blocks)
    out = jax.ShapeDtypeStruct((group // 2 * image_rows // 2, HEAD_DIM), jnp.float32)
    return pl.pallas_call(
        functools.partial(weigh_kernel, group, weight_row, image_rows),
        out_shape=[out] * 4,
        in_specs=[VMEM] * group,
        out_specs=[VMEM] * 4,
        compiler_params=SMALL,
        cost_estimate=NO_COST,
        name="weigh",
    )(*blocks)


def blend_kernel(count, *refs):
    sides, outs = refs[: 3 * count], refs[3 * count :]
    half, blocks = outs[0].shape[0], len(outs) // count
    for index, out in enumerate(outs):
        own, other, weight_ref = sides[index // blocks * 3 : index // blocks * 3 + 3]
        rows = pl.ds(index % blocks * half, half)
        for at_head in range(0, own.shape[1], HEAD_DIM):
            head = pl.ds(at_head, HEAD_DIM)
            weight = weight_ref[rows]
            mixed = weight * own[rows, head].astype(jnp.float32)
            mixed += (BLEND_TOTAL - weight) * other[rows, head].astype(jnp.float32)
            out[:, head] = (mixed * (1.0 / BLEND_TOTAL)).astype(jnp.bfloat16)


def blend_strips(sides, blocks):
    rows, width = sides[0][0].shape
    out = jax.ShapeDtypeStruct((len(sides) * rows // blocks, width), jnp.bfloat16)
    return pl.pallas_call(
        functools.partial(blend_kernel, len(sides)),
        out_shape=[out] * blocks,
        in_specs=[VMEM] * (3 * len(sides)),
        out_specs=[VMEM] * blocks,
        compiler_params=SMALL,
        cost_estimate=NO_COST,
        name="blend",
    )(*sum(sides, ()))


def load_kernel(w_out, *refs):
    out, sem = refs[-2:]
    copy = pltpu.make_async_copy(w_out, out, sem)
    copy.start()
    copy.wait()


def load_weights(w_out, after):
    return pl.pallas_call(
        load_kernel,
        out_shape=jax.ShapeDtypeStruct(w_out.shape, w_out.dtype),
        in_specs=[ANY] * (1 + len(after)),
        out_specs=VMEM,
        scratch_shapes=[pltpu.SemaphoreType.DMA],
        compiler_params=SMALL,
        cost_estimate=NO_COST,
        name="load_weights",
    )(w_out, *after)


def hold_kernel(source, *refs):
    refs[-1][...] = source[...]


def hold(array, after):
    return pl.pallas_call(
        hold_kernel,
        out_shape=jax.ShapeDtypeStruct(array.shape, array.dtype),
        in_specs=[VMEM] + [ANY] * len(after),
        out_specs=VMEM,
        compiler_params=SMALL,
        cost_estimate=NO_COST,
        name="hold",
    )(array, *after)


def collect_kernel(group, *refs):
    blocks, out = refs[:group], refs[-1]
    width = blocks[0].shape[1]
    for distance in range(group):
        start = pl.multiple_of(partner(distance, group) * width, HEAD_DIM)
        out[:, pl.ds(start, width)] = blocks[distance][...]


def collect(blocks):
    group = len(blocks)
    rows, width = blocks[0].shape
    return pl.pallas_call(
        functools.partial(collect_kernel, group),
        out_shape=jax.ShapeDtypeStruct((rows, group * width), blocks[0].dtype),
        in_specs=[VMEM] * group,
        out_specs=VMEM,
        compiler_params=SMALL,
        cost_estimate=NO_COST,
        name="collect",
    )(*blocks)


TILES = 6


def begin_kernel(left, right, weights, total, features):
    depth = features.shape[1]
    for row in range(features.shape[0] // WCOLS):
        strip = slice(row * STRIDE, (row + 1) * STRIDE)
        at = row * WCOLS
        features[at : at + STRIDE] = left[strip]
        features[at + STRIDE : at + WCOLS] = right[strip]
    tile = total.shape[1] // TILES
    for at in range(0, total.shape[1], tile):
        total[:, at : at + tile] = jnp.dot(
            features[...], weights[:depth, at : at + tile], preferred_element_type=jnp.float32
        )


def project_begin(left, right, weights):
    rows, depth = left.shape
    return pl.pallas_call(
        begin_kernel,
        out_shape=jax.ShapeDtypeStruct((2 * rows, weights.shape[1]), jnp.float32),
        in_specs=[VMEM] * 3,
        out_specs=VMEM,
        scratch_shapes=[pltpu.VMEM((2 * rows, depth), jnp.bfloat16)],
        compiler_params=SMALL,
        cost_estimate=NO_COST,
        name="project_begin",
    )(left, right, weights)


def end_kernel(left, right, first_in, second_in, *refs):
    weight_left, weight_right, weights, total, out, features, result, sems = refs
    rows = left.shape[0]
    even = lax.rem(lax.axis_index("win"), 2) == 0
    for side, (own, other, weight_ref) in enumerate(
        ((left, (second_in, first_in), weight_left), (right, (first_in, second_in), weight_right))
    ):
        weight = weight_ref[:rows]
        for at in range(0, own.shape[1], HEAD_DIM):
            head = pl.ds(at, HEAD_DIM)
            mixed = weight * own[:, head].astype(jnp.float32)
            theirs = [ref[:, head].astype(jnp.float32) for ref in other]
            mixed += (BLEND_TOTAL - weight) * jnp.where(even, *theirs)
            mixed = (mixed * (1.0 / BLEND_TOTAL)).astype(jnp.bfloat16)
            for row in range(rows // STRIDE):
                start = row * WCOLS + side * STRIDE
                features[pl.ds(start, STRIDE), head] = mixed[row * STRIDE : (row + 1) * STRIDE]
    tile = result.shape[1] // TILES
    first = weights.shape[0] - features.shape[1]
    copies = []
    for at in range(0, result.shape[1], tile):
        columns = pl.ds(at, tile)
        product = jnp.dot(
            features[...], weights[first:, at : at + tile], preferred_element_type=jnp.float32
        )
        result[:, columns] = (total[:, columns] + product).astype(jnp.bfloat16)
        copy = pltpu.make_async_copy(
            result.at[:, columns], out.at[:, columns], sems.at[len(copies)]
        )
        copy.start()
        copies.append(copy)
    for copy in copies:
        copy.wait()


def project_end(strips, blend_weights, weights, total):
    rows, width = total.shape
    return pl.pallas_call(
        end_kernel,
        out_shape=jax.ShapeDtypeStruct((rows, width), jnp.bfloat16),
        in_specs=[VMEM] * 8,
        out_specs=ANY,
        scratch_shapes=[
            pltpu.VMEM((rows, strips[0].shape[1]), jnp.bfloat16),
            pltpu.VMEM((rows, width), jnp.bfloat16),
            pltpu.SemaphoreType.DMA((TILES,)),
        ],
        compiler_params=SMALL,
        cost_estimate=NO_COST,
        name="project_end",
    )(*strips, *blend_weights, weights, total)


def absorb(carried, keys, values, valid_keys, queries):
    running, denominator, numerator = carried
    scores = jnp.einsum("qhd,khd->qhk", queries, keys, preferred_element_type=jnp.float32) * SCALE
    scores = jnp.where(valid_keys[None, None, :], scores, -jnp.inf)
    updated = jnp.maximum(running, jnp.max(scores, axis=2))
    rescale = jnp.exp(running - updated)
    weights = jnp.exp(scores - updated[:, :, None])
    denominator = denominator * rescale + jnp.sum(weights, axis=2)
    product = jnp.einsum(
        "qhk,khd->qhd", weights.astype(jnp.bfloat16), values, preferred_element_type=jnp.float32
    )
    numerator = numerator * rescale[:, :, None] + product
    return (updated, denominator, numerator)


def attend_ring(blocks, query_blocks, prompt_ids, image_rows, text_rows):
    group, width = len(blocks), blocks[0].shape[1]
    head_count = width // HEAD_DIM
    key_rows = image_rows + text_rows
    queries = jnp.concatenate([block[:image_rows] for block in blocks[:query_blocks]], axis=0)
    starts = [image_rows if d < query_blocks else 0 for d in range(group)]
    keys, values = (
        jnp.concatenate(
            [block[at + s : at + s + key_rows] for block, s in zip(blocks, starts)], axis=0
        ).reshape(-1, head_count, HEAD_DIM)
        for at in (0, key_rows)
    )
    queries = queries.reshape(-1, head_count, HEAD_DIM)
    seq_count = lax.axis_size("seq")
    group_count = seq_count // group
    own_group = lax.axis_index("seq") // group
    order = (lax.axis_index("seq") % group) ^ jnp.arange(group)
    text_valid = prompt_ids.reshape(seq_count, text_rows) != 0

    def valid_for(source):
        text = lax.dynamic_slice_in_dim(text_valid, source * group, group, 0)[order]
        return jnp.concatenate([jnp.ones((group, image_rows), jnp.bool_), text], axis=1).reshape(-1)

    query_count = queries.shape[0]
    initial = (
        jnp.full((query_count, head_count), -jnp.inf, jnp.float32),
        jnp.zeros((query_count, head_count), jnp.float32),
        jnp.zeros((query_count, head_count, HEAD_DIM), jnp.float32),
    )
    carried = absorb(initial, keys, values, valid_for(own_group), queries)

    def one_turn(turn, state):
        current, keys, values = state
        keys, values = shifted(keys, "seq", group), shifted(values, "seq", group)
        source = (own_group - turn) % group_count
        return (absorb(current, keys, values, valid_for(source), queries), keys, values)

    carried, _, _ = lax.fori_loop(1, group_count, one_turn, (carried, keys, values))
    _, denominator, numerator = carried
    attended = (numerator / denominator[:, :, None]).astype(jnp.bfloat16)
    return attended.reshape(query_blocks, image_rows, width)


def ring_strips(blocks, prompt_ids, image_rows, text_rows):
    group = len(blocks)
    attended = attend_ring(blocks, group, prompt_ids, image_rows, text_rows)
    sides = attended.reshape(2, -1, 2, STRIDE, attended.shape[2])
    return [[sides[p, :, s].reshape(-1, attended.shape[2]) for p in range(2)] for s in range(2)]


def ring_half(blocks, prompt_ids, image_rows, text_rows):
    return list(attend_ring(blocks, len(blocks) // 2, prompt_ids, image_rows, text_rows))


def on_device(query, key_image, value_image, key_text, value_text, prompt_ids, blend, w_out):
    seq_count = lax.axis_size("seq")
    group = math.gcd(HEADS & -HEADS, seq_count)
    heads = HEADS // group - 1
    halfway = group // 2
    image_rows, text_rows = query.shape[1], key_text.shape[1]
    message_rows = 3 * image_rows + 2 * text_rows
    sources = [query[0], key_image[0], key_text[0], value_image[0], value_text[0]]
    sources = [pltpu.with_memory_space_constraint(source, pltpu.HBM) for source in sources]

    blend_there = pltpu.with_memory_space_constraint(blend, pltpu.HBM)
    far, near = tuple(range(halfway, group)), tuple(range(1, halfway))
    received = [None] * group
    for distances in (far, near):
        packed = pack(sources, blend_there, heads, group, distances)
        for distance, message in zip(distances, packed):
            received[distance] = swapped(message, distance)
    weights = load_weights(w_out, [])
    prepared = prepare(sources, blend, prompt_ids, heads, group, [weights])
    received[0], packed, bias = prepared[0], prepared[1:-1], prepared[-1]
    first = received
    second = [packed[0]] + [swapped(hold(packed[d], [first[halfway]]), d) for d in near]
    for distance in far:
        second.append(swapped(hold(packed[distance], first[halfway:] if distance == halfway else []), distance))
    blend_weights = weigh(first, message_rows, image_rows)

    def strips_of(blocks):
        if seq_count == group:
            return attend(blocks, bias, image_rows, text_rows)
        return ring_strips(blocks, prompt_ids[0], image_rows, text_rows)

    def results_of(blocks, after):
        if seq_count == group:
            return attend_half(blocks, bias, image_rows, text_rows, after)
        return ring_half(blocks, prompt_ids[0], image_rows, text_rows)

    def returned(mixed):
        return [mixed[0]] + [swapped(mixed[d], d) for d in range(1, len(mixed))]

    lefts, rights = strips_of(first)
    sides = [
        (left, shifted(right, "win", 1), weight)
        for left, right, weight in zip(lefts, rights, blend_weights[::2])
    ]
    mixed = blend_strips(sides, group)
    begun = returned(mixed)

    results = returned(results_of(second, [mixed[0], weights]))
    left, right, to_first, to_second = merge(results, group)
    second_in, first_in = paired(to_second, True), paired(to_first, False)
    begins = collect(begun)
    total = project_begin(begins, shifted(begins, "win", -1), weights)
    strips = [left, right, first_in, second_in]
    return project_end(strips, blend_weights[:2], weights, total)[None]


def solution(mesh):
    tokens = P(("pano", "win"), "seq", None)
    return jax.shard_map(
        on_device,
        mesh=mesh,
        in_specs=(tokens,) * 5 + (P(("pano", "win"), None), P(("pano", "win"), "seq"), P()),
        out_specs=tokens,
        check_vma=False,
    )
```
